128 devices in a mesh: dp: 2 (over y_hi), blk: 8 (over x, core), heads: 8 (over y_lo, z).
Axes of the slice: x: 4, y: 4 (y_hi: 2, y_lo: 2; y = y_hi * 2 + y_lo), z: 4, core: 2. Of those that a mesh axis runs over, the one named last changes fastest.
Arguments:
- tokens: bfloat16 [2, 8192, 4096], P('dp', ('blk', 'heads')), may hold values from -24 to 24
- norm_gain: float32 [4096], replicated, may hold values from 0.5 to 1.5
- segment_ids: int32 [2, 8192], P('dp', ('blk', 'heads')), may hold values from 0 to 7, never falling along the last dimension, each value on 1 to 4096 neighbouring positions
- w_query: bfloat16 [4096, 4096], P(None, 'heads'), may hold values from -2 to 2
- w_key: bfloat16 [4096, 1024], P(None, 'heads'), may hold values from -2 to 2
- w_value: bfloat16 [4096, 1024], P(None, 'heads'), may hold values from -0.09375 to 0.09375
- w_out: bfloat16 [4096, 4096], P('heads'), may hold values from -1 to 1
Outputs:
- attn_delta: bfloat16 [2, 8192, 4096], P('dp', ('blk', 'heads'))
- input_gram: float32 [4096, 4096], P(('dp', 'blk', 'heads'))
The draws below stay inside these ranges and needn't reach their ends.
Inputs may be any that keep to these rules, and one draw needn't show every extreme that they name: `segment_ids`: segment numbers never fall along a sequence; a document holds at most 4096 positions, and one holds exactly that many.
All inputs are finite; a program needn't handle non-finite values.
Results may differ from the reference program's by a relative error of at most 0.02.
Values may be sent and summed in bfloat16 or wider, within the bound.
A program may use at most 128 MiB of HBM per device.

```python
import math
import jax
import jax.numpy as jnp
import numpy as np
from jax import lax

D = 4096
HEADS = 32
KVH = 8
HD = 128
SEGS = 8
SEQS = 2
L = 8192
N_HEADS = 8


def draw_tokens(key, part):
    key = jax.random.fold_in(key, 3)
    key_one = jax.random.fold_in(key, 0)
    return jnp.clip(jax.random.normal(key_one, (SEQS, L, D), jnp.float32), -6.0, 6.0).astype(jnp.bfloat16)


def draw_w_query(key, part):
    key = jax.random.fold_in(key, 5)
    noise_part = jax.random.normal(key, (D, HEADS * HD), jnp.float32) * D ** (-0.5)
    return jnp.clip(noise_part, -2.0, 2.0).astype(jnp.bfloat16)


def draw_w_key(key, part):
    key = jax.random.fold_in(key, 7)
    noise_part = jax.random.normal(key, (D, KVH * HD), jnp.float32) * D ** (-0.5)
    return jnp.clip(noise_part, -2.0, 2.0).astype(jnp.bfloat16)


def level_of(rng, shape, cuts, smallest, high):
    factor_of = 1.0
    for axis_at, blocks in cuts:
        draws = jax.random.uniform(jax.random.fold_in(jax.random.fold_in(rng, 6), axis_at), (blocks,), jnp.float32, smallest / len(cuts), high / len(cuts))
        factor_of = factor_of * jnp.repeat(jnp.exp(draws), shape[axis_at] // blocks).reshape((-1,) + (1,) * (len(shape) - 1 - axis_at))
    return factor_of


def length_profile(amount, total, reach, skew):
    loads = [(1 << 20) // math.isqrt(standing ** skew) + 1 for standing in range(2, amount + 1)]
    rest, given = total - reach - (amount - 1), [1] * (amount - 1)
    while rest > 0:
        candidates = [i for i in range(amount - 1) if given[i] < reach]
        pool, remaining = sum([loads[i] for i in candidates]), rest
        for i in candidates:
            extra = min(reach - given[i], max(1, remaining * loads[i] // pool), rest)
            given[i] = given[i] + extra
            rest = rest - extra
    return np.array([reach] + given)


def ragged(own_key, amount, total, bound, lean):
    if amount == 2:
        one = jax.random.randint(own_key, (), max(1, total - bound), min(bound, total - 1) + 1)
        return jnp.stack([one, total - one])
    lengths = jnp.asarray(length_profile(amount, total, bound, lean), jnp.int32)
    twos = (amount - 1) // 2
    donor, sink = lengths[1:1 + 2 * twos:2], lengths[2:2 + 2 * twos:2]
    slack = jnp.minimum(donor - 1, bound - sink)
    passed = jax.random.randint(jax.random.fold_in(own_key, 1), (twos,), 0, 1 << 20) % (slack + 1)
    lengths = lengths.at[1:1 + 2 * twos:2].set(donor - passed).at[2:2 + 2 * twos:2].set(sink + passed)
    return lengths[jax.random.permutation(jax.random.fold_in(own_key, 2), amount)]


def gaussian(own_key, dims, width, limit, cuts=(), kind=jnp.bfloat16):
    drawn = jax.random.normal(own_key, dims, jnp.float32) * width
    if len(cuts) > 0:
        drawn = level_of(own_key, dims, cuts, -0.22, 0.18) * drawn
    return jnp.clip(drawn, min=-limit, max=limit).astype(kind)


def setup_inputs(seed: int = 0) -> dict:
    key_list = jax.random.split(jax.random.key(seed), 8)
    return {
        "tokens": draw_tokens(jax.random.fold_in(key_list[7], 71), 0),
        "norm_gain": jnp.clip(1.0 + 0.1 * jax.random.normal(key_list[1], (D,), jnp.float32), 0.5, 1.5),
        "segment_ids": jax.vmap(lambda own: jnp.searchsorted(jnp.cumsum(ragged(own, SEGS, L, L // 2, 0)), jnp.arange(L), side="right"))(jax.random.split(key_list[2], SEQS)).reshape((SEQS, L)).astype(jnp.int32),
        "w_query": draw_w_query(jax.random.fold_in(key_list[7], 71), 0),
        "w_key": draw_w_key(jax.random.fold_in(key_list[7], 71), 0),
        "w_value": gaussian(key_list[5], (D, KVH * HD), D ** -0.5, 0.09375, ((1, 8),)),
        "w_out": gaussian(key_list[6], (HEADS * HD, D), (HD // 4) ** -0.5, 1.0, ((0, 8),)),
    }


EPSILON = 1e-05
ROPE_BASE = 500000.0
NEGATIVE = -1e+30

def rotate(values, positions):
    head_width = values.shape[-1]
    half_width = head_width // 2
    frequency = ROPE_BASE ** (-(jnp.arange(half_width, dtype=jnp.float32) * 2.0 / head_width))
    angles = positions[:, None] * frequency[None, :]
    cosine = jnp.cos(angles)[:, None, :]
    sine_part = jnp.sin(angles)[:, None, :]
    lower_half = values[..., :half_width]
    upper_half = values[..., half_width:]
    return jnp.concatenate([lower_half * cosine - upper_half * sine_part, upper_half * cosine + lower_half * sine_part], -1)

def reference(tokens, norm_gain, segment_ids, w_query, w_key, w_value, w_out):
    inputs = tokens.astype(jnp.float32)
    mean_square = lax.optimization_barrier(jnp.mean(inputs * inputs, axis=-1, keepdims=True))
    normed = (inputs * lax.rsqrt(mean_square + EPSILON) * norm_gain).astype(jnp.bfloat16)
    flat_rows = normed.reshape(SEQS * L, D)
    input_gram = jnp.dot(flat_rows.T, flat_rows, preferred_element_type=jnp.float32) / (SEQS * L)
    group_size = HEADS // KVH
    block_len = math.gcd(L, 1024)
    block_count = L // block_len
    positions = jnp.arange(L, dtype=jnp.float32)
    key_index = jnp.arange(L, dtype=jnp.int32)
    score_scale = 1.0 / math.sqrt(HD)
    group_width = HEADS * HD // N_HEADS
    deltas = []
    for sequence in range(SEQS):
        seq_rows = normed[sequence]
        queries = rotate(jnp.dot(seq_rows, w_query, preferred_element_type=jnp.float32).reshape(L, HEADS, HD), positions).astype(jnp.bfloat16)
        key_heads = rotate(jnp.dot(seq_rows, w_key, preferred_element_type=jnp.float32).reshape(L, KVH, HD), positions).astype(jnp.bfloat16)
        value_heads = jnp.dot(seq_rows, w_value, preferred_element_type=jnp.float32).astype(jnp.bfloat16).reshape(L, KVH, HD)
        seg_ids = segment_ids[sequence]

        def attend_block(work_item):
            head_num = work_item // block_count
            row_anchor = work_item % block_count * block_len
            head_queries = lax.dynamic_index_in_dim(queries, head_num, 1, keepdims=False)
            query_rows = lax.dynamic_slice_in_dim(head_queries, row_anchor, block_len, 0)
            key_rows = lax.dynamic_index_in_dim(key_heads, head_num // group_size, 1, keepdims=False)
            val_rows = lax.dynamic_index_in_dim(value_heads, head_num // group_size, 1, keepdims=False)
            scores = jnp.dot(query_rows, key_rows.T, preferred_element_type=jnp.float32) * score_scale
            query_seg = lax.dynamic_slice_in_dim(seg_ids, row_anchor, block_len, 0)
            query_index = row_anchor + jnp.arange(block_len, dtype=jnp.int32)
            allowed = (query_seg[:, None] == seg_ids[None, :]) & (key_index[None, :] <= query_index[:, None])
            row_max = lax.optimization_barrier(jnp.max(jnp.where(allowed, scores, NEGATIVE), axis=1, keepdims=True))
            exponent = jnp.where(allowed, jnp.exp(scores - row_max), 0.0)
            row_total = lax.optimization_barrier(jnp.sum(exponent, axis=1, keepdims=True))
            mixed = jnp.dot(exponent.astype(jnp.bfloat16), val_rows, preferred_element_type=jnp.float32)
            return (mixed / row_total).astype(jnp.bfloat16)
        blocks = lax.map(attend_block, jnp.arange(HEADS * block_count, dtype=jnp.int32))
        attended = blocks.reshape(HEADS, L, HD).transpose(1, 0, 2).reshape(L, HEADS * HD)
        delta_sum = jnp.zeros((L, D), jnp.float32)
        for head_group in range(N_HEADS):
            head_cols = attended[:, head_group * group_width:(head_group + 1) * group_width]
            partial_value = jnp.dot(head_cols, w_out[head_group * group_width:(head_group + 1) * group_width], preferred_element_type=jnp.float32).astype(jnp.bfloat16)
            partial_value = lax.optimization_barrier(partial_value)
            delta_sum = delta_sum + partial_value.astype(jnp.float32)
        deltas.append(delta_sum.astype(jnp.bfloat16))
    return (jnp.stack(deltas), input_gram)
```

```python
import math

import jax
import jax.numpy as jnp
import numpy as np
from jax import lax
from jax.experimental import pallas as pl
from jax.experimental.pallas import tpu as pltpu
from jax.sharding import PartitionSpec as P

MESH = pl.DeviceIdType.MESH
HD = 128
D = 4096
ROWS = 128
EPSILON = 1e-05
ROPE_BASE = 500000.0
BIG = 1e30
FEATS = 16
KROWS = HD + FEATS
PAD = 4
F32 = jnp.float32
BF16 = jnp.bfloat16


def tables():
    frequency = ROPE_BASE ** (-(np.arange(64, dtype=np.float64) * 2.0 / HD))
    frequency = np.concatenate([frequency, frequency])
    base = np.arange(64)[:, None] * float(ROWS) * frequency[None, :]
    step = np.arange(ROWS)[:, None] * frequency[None, :]
    return [f(v).astype(np.float32) for v in (base, step) for f in (np.cos, np.sin)]


def dot(a, b, dims=(((1,), (0,)), ((), ()))):
    return lax.dot_general(a, b, dims, preferred_element_type=F32)


def kernel(
    tok, gain, seg, wq_h, wk_h, wv_h, wo_h, base_cos, base_sin, step_cos, step_sin,
    out, gram,
    X, WQ, WKV, WO, QE, KV, PKT, GP, GC, GX, GD, AT, AR, PT, RA, RF, ACC, TOP,
    ss, rs, kss, krs, ls,
):
    a, b, h = lax.axis_index("dp"), lax.axis_index("blk"), lax.axis_index("heads")
    x, c = b // 2, b % 2
    y, z = h // 4, h % 4
    zp, zm, zo = (z + 1) % 4, (z + 3) % 4, (z + 2) % 4
    up, down = (a, b, y * 4 + zp), (a, b, y * 4 + zm)
    side = (a, b, (1 - y) * 4 + z)
    far = (1 - a, b, (1 - y) * 4 + z)
    twin = (a, x * 2 + 1 - c, h)
    other = (1 - a, b, h)
    ring = [None] + [(a, ((x + k) % 4) * 2 + c, h) for k in (1, 2, 3)]

    loads = [
        pltpu.make_async_copy(wk_h, WKV.at[:, 0:HD], ls.at[0]),
        pltpu.make_async_copy(wv_h, WKV.at[:, HD : 2 * HD], ls.at[1]),
        pltpu.make_async_copy(wq_h, WQ, ls.at[2]),
        pltpu.make_async_copy(wo_h, WO.at[0], ls.at[3]),
    ]
    for load in loads:
        load.start()

    barrier = pltpu.get_barrier_semaphore()
    partners = [up, down, side, far, twin, other] + ring[1:]
    for partner in partners:
        pl.semaphore_signal(barrier, inc=1, device_id=partner, device_id_type=MESH)

    def normalise(i, _):
        at = pl.ds(pl.multiple_of(i * 16, 16), 16)
        values = tok[at, :].astype(F32)
        mean_square = jnp.mean(values * values, axis=-1, keepdims=True)
        X[h, at, 0:D] = (values * lax.rsqrt(mean_square + EPSILON) * gain[...]).astype(BF16)
        return 0

    lax.fori_loop(0, ROWS // 16, normalise, 0)
    feature = lax.broadcasted_iota(jnp.int32, (ROWS, ROWS), 0)
    X[h, :, D : D + ROWS] = jnp.where(feature == seg[...], 1.0, 0.0).astype(BF16)

    pl.semaphore_wait(barrier, len(partners))

    def send(i, src, dst, device):
        return pltpu.make_async_remote_copy(
            src_ref=src, dst_ref=dst, send_sem=ss.at[i], recv_sem=rs.at[i],
            device_id=device, device_id_type=MESH,
        )

    def slab(g, half=None):
        return X.at[g] if half is None else X.at[g, pl.ds(half * 64, 64)]

    hs = (1 - y) * 4 + z
    own_side = send(0, X.at[h], X.at[h], side)
    own_up = send(1, X.at[h], X.at[h], up)
    own_down = send(2, X.at[h], X.at[h], down)
    oth_up = send(3, X.at[hs], X.at[hs], up)
    oth_down = send(4, X.at[hs], X.at[hs], down)
    fw = []
    for k, col in enumerate((y, 1 - y)):
        fw.append(send(5 + 2 * k, slab(col * 4 + zm, 0), slab(col * 4 + zm, 0), up))
        fw.append(send(6 + 2 * k, slab(col * 4 + zp, 1), slab(col * 4 + zp, 1), down))
    own_side.start()
    own_up.start()
    own_down.start()
    half_rows = pl.ds(pl.multiple_of(c * 256, 256), 256)
    wo_far = send(9, wo_h.at[half_rows], WO.at[1, half_rows], far)
    wo_far.start()
    wo_twin = send(10, WO.at[1, half_rows], WO.at[1, half_rows], twin)

    pads = lax.broadcasted_iota(jnp.int32, (FEATS, HD), 0)
    for slot in range(PAD):
        KV[slot] = jnp.zeros((KROWS + HD, HD), BF16)
        KV[slot, HD:KROWS, :] = jnp.where(pads == 8, 1.0, 0.0).astype(BF16)

    def chunk_of(i):
        stage, second = i // 2, i % 2
        col = jnp.where(stage == 0, jnp.where(second == 0, y, 1 - y),
              jnp.where(stage == 1, y,
              jnp.where(stage == 2, 1 - y, jnp.where(second == 0, y, 1 - y))))
        row = jnp.where(stage == 0, z, jnp.where(stage == 3, zo, jnp.where(second == 0, zm, zp)))
        return col * 4 + row

    def kv_copy(kind, i):
        g = chunk_of(i)
        quad = [x, x, x, (x + 3) % 4, (x + 2) % 4][kind]
        device = [twin, ring[1], ring[2], twin, twin][kind]
        slot = (quad * 2 + c) * 8 + g + PAD
        return pltpu.make_async_remote_copy(
            src_ref=KV.at[slot], dst_ref=KV.at[slot], send_sem=kss.at[kind, i],
            recv_sem=krs.at[kind, i], device_id=device, device_id_type=MESH,
        )

    lane = lax.broadcasted_iota(jnp.int32, (ROWS, HD), 1)
    scale = math.log2(math.e) / math.sqrt(HD)

    def project(stage):
        ga, gb = chunk_of(2 * stage), chunk_of(2 * stage + 1)
        rows = jnp.concatenate([X[ga, :, 0:D], X[gb, :, 0:D]], axis=0)
        pair = (ga, gb)
        turns = []
        for g in pair:
            rc = b * 8 + g
            bc, bs = base_cos[pl.ds(rc, 1), :], base_sin[pl.ds(rc, 1), :]
            cosine = bc * step_cos[...] - bs * step_sin[...]
            sine = bs * step_cos[...] + bc * step_sin[...]
            turns.append((cosine, jnp.where(lane < 64, -sine, sine)))
        kv = dot(rows, WKV[...])
        for k, g in enumerate(pair):
            cosine, sine = turns[k]
            slot = b * 8 + g + PAD
            key = kv[k * ROWS : (k + 1) * ROWS, 0:HD]
            key = key * cosine + pltpu.roll(key, 64, 1) * sine
            KV[slot, 0:HD, :] = key.T.astype(BF16)
            KV[slot, HD:KROWS, :] = X[g, 0:FEATS, D : D + ROWS]
            KV[slot, KROWS : KROWS + HD, :] = kv[k * ROWS : (k + 1) * ROWS, HD : 2 * HD].astype(BF16)
        for i in (0, 1):
            for kind in range(3):
                kv_copy(kind, 2 * stage + i).start()
        for n in range(2):
            part = dot(rows, WQ[:, n * 256 : (n + 1) * 256])
            for k, g in enumerate(pair):
                cosine, sine = turns[k]
                for m in range(2):
                    head = part[k * ROWS : (k + 1) * ROWS, m * HD : (m + 1) * HD]
                    head = (head * cosine + pltpu.roll(head, 64, 1) * sine) * scale
                    at = (n * 2 + m) * ROWS
                    QE[g, at : at + ROWS, 0:HD] = head.astype(BF16)
        for g in pair:
            mine = X[g, :, D : D + ROWS].astype(F32).T
            ext = jnp.where(lane < 8, jnp.where(mine > 0.5, 0.0, -BIG), jnp.where(lane == 8, -BIG, 0.0))
            for m in range(4):
                QE[g, m * ROWS : (m + 1) * ROWS, HD : 2 * HD] = ext.astype(BF16)

    def forward_kv(stage):
        for i in (0, 1):
            for kind in (1, 2):
                kv_copy(kind, 2 * stage + i).wait_recv()
                kv_copy(kind + 2, 2 * stage + i).start()

    for load in loads[:3]:
        load.wait()

    def gather_stage(stage, _):
        @pl.when(stage == 0)
        def _():
            own_side.wait_recv()
            oth_up.start()
            oth_down.start()

        @pl.when(stage == 1)
        def _():
            own_up.wait_recv()
            fw[0].start()
            own_down.wait_recv()
            fw[1].start()

        @pl.when(stage == 2)
        def _():
            oth_up.wait_recv()
            fw[2].start()
            oth_down.wait_recv()
            fw[3].start()

        @pl.when(stage == 3)
        def _():
            for copy in fw:
                copy.wait_recv()

        project(stage)

        @pl.when(stage > 0)
        def _():
            forward_kv(stage - 1)

        return 0

    lax.fori_loop(0, 4, gather_stage, 0)

    wo_far.wait_recv()
    wo_twin.start()
    pick_row = lax.broadcasted_iota(jnp.int32, (128, 512), 0)
    pick_col = lax.broadcasted_iota(jnp.int32, (128, 512), 1)
    chosen = (pick_col == (pick_row // 32) * 128 + z * 32 + pick_row % 32)
    chosen = jnp.where(chosen, 1.0, 0.0).astype(BF16)

    for group in range(4):
        parts = []
        for n in range(4):
            q = (n % 2) * 8 + (2 * (group % 2) + n // 2) * 2 + group // 2
            at = pl.ds(pl.multiple_of(q * 256 + y * 128, 128), 128)
            parts.append(X[:, :, at].reshape(1024, 128))
        taken = jnp.concatenate(parts, axis=1)
        PKT[group * 128 : (group + 1) * 128, :] = dot(chosen, taken, (((1,), (1,)), ((), ()))).astype(BF16)

    def gram_tile(n, _):
        at = pl.ds(pl.multiple_of(n * 256, 256), 256)
        tile = dot(PKT[...], X[:, :, at].reshape(1024, 256)).astype(BF16)
        GP[0, :, at] = tile[0:256]
        GP[1, :, at] = tile[256:512]
        return 0

    lax.fori_loop(0, 16, gram_tile, 0)
    gram_twin = send(11, GP.at[1 - c], GC, twin)
    gram_twin.start()
    gram_ring = [None] + [
        send(11 + k, GP.at[c, pl.ds(pl.multiple_of(((x + k) % 4) * 64, 64), 64)], GX.at[k - 1], ring[k])
        for k in (1, 2, 3)
    ]
    gram_other = send(15, GC.at[pl.ds(pl.multiple_of((1 - a) * 32, 32), 32)], GD, other)

    forward_kv(3)

    def settle(i, _):
        kv_copy(0, i).wait_recv()
        kv_copy(3, i).wait_recv()
        kv_copy(4, i).wait_recv()
        return 0

    lax.fori_loop(0, 8, settle, 0)
    wo_twin.wait_recv()
    loads[3].wait()

    tri = lax.broadcasted_iota(jnp.int32, (512, HD), 0) % ROWS >= lax.broadcasted_iota(jnp.int32, (512, HD), 1)
    blank = jnp.zeros((256 - KROWS, HD), BF16)
    ones = jnp.ones((HD, HD), BF16)

    def attend(g):
        pc = b * 8 + g
        slot = pc + PAD
        keys = jnp.concatenate([KV[slot, 0:KROWS, :], blank], axis=0)
        scores = jnp.where(tri, dot(QE[g], keys), -BIG)
        top = jnp.max(scores, axis=1, keepdims=True)
        probs = jnp.exp2(scores - top).astype(BF16)
        ACC[...] = dot(probs, jnp.concatenate([KV[slot, KROWS : KROWS + HD, :], ones], axis=1))
        TOP[...] = jnp.broadcast_to(top, (512, HD))

        def step(t, _):
            first = slot - 4 * (t + 1)
            keys = jnp.concatenate(
                [jnp.concatenate([KV[first + j, 0:KROWS, :], blank], axis=0) for j in range(4)], axis=1)
            values = jnp.concatenate(
                [jnp.concatenate([KV[first + j, KROWS : KROWS + HD, :], ones], axis=1) for j in range(4)], axis=0)
            scores = dot(QE[g], keys)
            before = TOP[:, 0:1]
            top = jnp.maximum(before, jnp.max(scores, axis=1, keepdims=True))
            probs = jnp.exp2(scores - top).astype(BF16)
            ACC[...] = ACC[...] * jnp.exp2(before - top) + dot(probs, values)
            TOP[...] = jnp.broadcast_to(top, (512, HD))
            return 0

        lax.fori_loop(0, jnp.minimum(8, (pc + 3) // 4), step, 0)
        mixed = (ACC[:, 0:HD] / ACC[:, HD : 2 * HD]).astype(BF16)
        for m in range(4):
            AT[g, :, m * HD : (m + 1) * HD] = mixed[m * ROWS : (m + 1) * ROWS]

    turned = [
        send(16, PT.at[0, pl.ds(0, 64)], RA.at[0], up),
        send(17, PT.at[0, pl.ds(64, 64)], RA.at[1], down),
        send(18, PT.at[1], RF.at[0], up),
        send(19, PT.at[2], RF.at[1], down),
    ]

    def row_of(k):
        return jnp.where(k == 0, zo, jnp.where(k == 1, zp, jnp.where(k == 2, zm, z)))

    def swap(k):
        return pltpu.make_async_remote_copy(
            src_ref=AT.at[(1 - y) * 4 + row_of(k)], dst_ref=AR.at[k], send_sem=ss.at[20 + k],
            recv_sem=rs.at[20 + k], device_id=side, device_id_type=MESH,
        )

    def out_stage(k, _):
        row = row_of(k)

        def both(i, _):
            attend(jnp.where(i == 0, 1 - y, y) * 4 + row)

            @pl.when(i == 0)
            def _():
                swap(k).start()

            return 0

        lax.fori_loop(0, 2, both, 0)
        swap(k).wait_recv()

        def out_tile(n, _):
            at = pl.ds(pl.multiple_of(n * 512, 512), 512)
            PT[k, :, at] = (dot(AT[y * 4 + row], WO[0, :, at]) + dot(AR[k], WO[1, :, at])).astype(BF16)
            return 0

        lax.fori_loop(0, 8, out_tile, 0)

        @pl.when(k == 0)
        def _():
            turned[0].start()
            turned[1].start()
            gram_twin.wait_recv()

            def add(n, _):
                at = pl.ds(pl.multiple_of(n * 512, 512), 512)
                GP[c, :, at] = (GP[c, :, at].astype(F32) + GC[:, at].astype(F32)).astype(BF16)
                return 0

            lax.fori_loop(0, 8, add, 0)
            for k in (1, 2, 3):
                gram_ring[k].start()

        for which in (0, 1):
            @pl.when(k == 1 + which)
            def _(which=which):
                turned[which].wait_recv()
                at = pl.ds(64 * which, 64)
                PT[1 + which, at] = (PT[1 + which, at].astype(F32) + RA[which].astype(F32)).astype(BF16)
                turned[2 + which].start()

        @pl.when(k == 2)
        def _():
            for k in (1, 2, 3):
                gram_ring[k].wait_recv()

            def add(n, _):
                at = pl.ds(pl.multiple_of(n * 512, 512), 512)
                total = GP[c, pl.ds(pl.multiple_of(x * 64, 64), 64), at].astype(F32)
                for k in range(3):
                    total = total + GX[k, :, at].astype(F32)
                GC[0:64, at] = total.astype(BF16)
                return 0

            lax.fori_loop(0, 8, add, 0)
            gram_other.start()

        return 0

    lax.fori_loop(0, 4, out_stage, 0)
    gram_other.wait_recv()
    mine = pl.ds(pl.multiple_of(a * 32, 32), 32)
    gram[...] = (GC[mine, :].astype(F32) + GD[...].astype(F32)) * (1.0 / 16384.0)
    turned[2].wait_recv()
    turned[3].wait_recv()
    out[...] = (PT[3].astype(F32) + RF[0].astype(F32) + RF[1].astype(F32)).astype(BF16)

    for copy in [own_side, own_up, own_down, oth_up, oth_down, *fw, wo_far, wo_twin, gram_twin,
                 *gram_ring[1:], gram_other, *turned]:
        copy.wait_send()

    def drain(i, _):
        for kind in range(5):
            kv_copy(kind, i).wait_send()
        return 0

    lax.fori_loop(0, 8, drain, 0)

    def drain_swap(k, _):
        swap(k).wait_send()
        return 0

    lax.fori_loop(0, 4, drain_swap, 0)


def per_device(tokens, norm_gain, segment_ids, w_query, w_key, w_value, w_out):
    vmem = pl.BlockSpec(memory_space=pltpu.VMEM)
    hbm = pl.BlockSpec(memory_space=pl.ANY)
    dma = pltpu.SemaphoreType.DMA
    scratch = [
        pltpu.VMEM((8, ROWS, D + ROWS), BF16),
        pltpu.VMEM((D, 512), BF16),
        pltpu.VMEM((D, 256), BF16),
        pltpu.VMEM((2, 512, D), BF16),
        pltpu.VMEM((8, 512, 256), BF16),
        pltpu.VMEM((64 + PAD, KROWS + HD, HD), BF16),
        pltpu.VMEM((512, 1024), BF16),
        pltpu.VMEM((2, 256, D), BF16),
        pltpu.VMEM((256, D), BF16),
        pltpu.VMEM((3, 64, D), BF16),
        pltpu.VMEM((32, D), BF16),
        pltpu.VMEM((8, ROWS, 512), BF16),
        pltpu.VMEM((4, ROWS, 512), BF16),
        pltpu.VMEM((4, ROWS, D), BF16),
        pltpu.VMEM((2, 64, D), BF16),
        pltpu.VMEM((2, ROWS, D), BF16),
        pltpu.VMEM((512, 256), F32),
        pltpu.VMEM((512, HD), F32),
        dma((24,)),
        dma((24,)),
        dma((5, 8)),
        dma((5, 8)),
        dma((4,)),
    ]
    delta, gram = pl.pallas_call(
        kernel,
        out_shape=(jax.ShapeDtypeStruct((ROWS, D), BF16), jax.ShapeDtypeStruct((32, D), F32)),
        in_specs=[vmem, vmem, vmem, hbm, hbm, hbm, hbm, vmem, vmem, vmem, vmem],
        out_specs=(vmem, vmem),
        scratch_shapes=scratch,
        compiler_params=pltpu.CompilerParams(
            collective_id=0, has_side_effects=True, vmem_limit_bytes=62 << 20),
        name="sublayer",
    )(tokens[0], norm_gain[None], segment_ids, w_query, w_key, w_value, w_out,
      *[jnp.asarray(t) for t in tables()])
    return delta[None], gram


def solution(mesh):
    return jax.shard_map(
        per_device,
        mesh=mesh,
        in_specs=(
            P("dp", ("blk", "heads"), None),
            P(),
            P("dp", ("blk", "heads")),
            P(None, "heads"),
            P(None, "heads"),
            P(None, "heads"),
            P("heads", None),
        ),
        out_specs=(P("dp", ("blk", "heads"), None), P(("dp", "blk", "heads"), None)),
        check_vma=False,
    )
```

```python
import math

import jax
import jax.numpy as jnp
import numpy as np
from jax import lax
from jax.experimental import pallas as pl
from jax.experimental.pallas import tpu as pltpu
from jax.sharding import PartitionSpec as P

MESH = pl.DeviceIdType.MESH
HD = 128
D = 4096
ROWS = 128
EPSILON = 1e-05
ROPE_BASE = 500000.0
BIG = 1e30
FEATS = 16
KROWS = HD + FEATS
PAD = 8
CUT = 18 * 128
WINDOW = 4096
F32 = jnp.float32
BF16 = jnp.bfloat16


def tables():
    frequency = ROPE_BASE ** (-(np.arange(64, dtype=np.float64) * 2.0 / HD))
    frequency = np.concatenate([frequency, frequency])
    base = np.arange(64)[:, None] * float(ROWS) * frequency[None, :]
    step = np.arange(ROWS)[:, None] * frequency[None, :]
    return [f(v).astype(np.float32) for v in (base, step) for f in (np.cos, np.sin)]


def dot(a, b, dims=(((1,), (0,)), ((), ()))):
    return lax.dot_general(a, b, dims, preferred_element_type=F32)


def kernel(
    tok, gain, seg, wq_h, wk_h, wv_h, wo_h, base_cos, base_sin, step_cos, step_sin,
    out, gram,
    X, WQ, WKV, WO, QE, KV, PKT, GP, GC, GX, GD, AT, AR, PT, RA, RF, ACC, TOP, S0, S1, M0, M1,
    ss, rs, kss, krs, sws, swr, ls,
):
    a, b, h = lax.axis_index("dp"), lax.axis_index("blk"), lax.axis_index("heads")
    x, c = b // 2, b % 2
    y, z = h // 4, h % 4
    zp, zm, zo = (z + 1) % 4, (z + 3) % 4, (z + 2) % 4
    up, down = (a, b, y * 4 + zp), (a, b, y * 4 + zm)
    side = (a, b, (1 - y) * 4 + z)
    far = (1 - a, b, (1 - y) * 4 + z)
    twin = (a, x * 2 + 1 - c, h)
    other = (1 - a, b, h)
    ring = [None] + [(a, ((x + k) % 4) * 2 + c, h) for k in (1, 2, 3)]

    loads = [
        pltpu.make_async_copy(wk_h, WKV.at[:, 0:HD], ls.at[0]),
        pltpu.make_async_copy(wv_h, WKV.at[:, HD : 2 * HD], ls.at[1]),
        pltpu.make_async_copy(wq_h, WQ, ls.at[2]),
        pltpu.make_async_copy(wo_h, WO.at[0], ls.at[3]),
    ]
    for load in loads:
        load.start()

    barrier = pltpu.get_barrier_semaphore()
    partners = [up, down, side, far, twin, other] + ring[1:]
    for partner in partners:
        pl.semaphore_signal(barrier, inc=1, device_id=partner, device_id_type=MESH)

    def normalise(i, _):
        at = pl.ds(pl.multiple_of(i * 16, 16), 16)
        values = tok[at, :].astype(F32)
        mean_square = jnp.mean(values * values, axis=-1, keepdims=True)
        X[h, at, 0:D] = (values * lax.rsqrt(mean_square + EPSILON) * gain[...]).astype(BF16)
        return 0

    lax.fori_loop(0, ROWS // 16, normalise, 0)
    feature = lax.broadcasted_iota(jnp.int32, (ROWS, ROWS), 0)
    X[h, :, D : D + ROWS] = jnp.where(feature == seg[...], 1.0, 0.0).astype(BF16)

    pl.semaphore_wait(barrier, len(partners))

    def send(i, src, dst, device):
        return pltpu.make_async_remote_copy(
            src_ref=src, dst_ref=dst, send_sem=ss.at[i], recv_sem=rs.at[i],
            device_id=device, device_id_type=MESH,
        )

    FIRST, LAST = pl.ds(0, CUT), pl.ds(CUT, D + ROWS - CUT)

    def move(i, g, columns, device, half=None):
        rows = pl.ds(0, ROWS) if half is None else pl.ds(half * 64, 64)
        return send(i, X.at[g, rows, columns], X.at[g, rows, columns], device)

    hs = (1 - y) * 4 + z
    om, op, oo = y * 4 + zm, y * 4 + zp, y * 4 + zo
    nm, np_ = (1 - y) * 4 + zm, (1 - y) * 4 + zp
    y_first = move(0, h, FIRST, side)
    y_last = move(1, h, LAST, side)
    z_first = [move(2, h, FIRST, up), move(3, h, FIRST, down)]
    z_last = [move(4, h, LAST, up), move(5, h, LAST, down)]
    n_first = [move(6, hs, FIRST, up), move(7, hs, FIRST, down)]
    half_first = [move(8, om, FIRST, up, 0), move(9, op, FIRST, down, 1)]
    half_last = [move(10, om, LAST, up, 0), move(11, op, LAST, down, 1)]
    y_near = [move(12, om, LAST, side), move(13, op, LAST, side)]
    y_oppo = [move(14, oo, LAST, side, 0), move(15, oo, LAST, side, 1)]
    half_next = [move(16, nm, FIRST, up, 0), move(17, np_, FIRST, down, 1)]
    gathers = [y_first, y_last, *z_first, *z_last, *n_first, *half_first, *half_last, *y_near, *y_oppo, *half_next]
    for copy in (y_first, *z_last, *z_first, y_last):
        copy.start()
    half_rows = pl.ds(pl.multiple_of(c * 256, 256), 256)
    wo_far = send(18, wo_h.at[half_rows], WO.at[1, half_rows], far)
    wo_far.start()
    wo_twin = send(19, WO.at[1, half_rows], WO.at[1, half_rows], twin)

    pads = lax.broadcasted_iota(jnp.int32, (FEATS, HD), 0)
    def clear(slot, _):
        KV[slot] = jnp.zeros((KROWS + HD, HD), BF16)
        KV[slot, HD:KROWS, :] = jnp.where(pads == 8, 1.0, 0.0).astype(BF16)
        return 0

    lax.fori_loop(0, PAD, clear, 0)

    def chunk_of(i):
        stage, second = i // 2, i % 2
        col = jnp.where(stage == 0, jnp.where(second == 0, y, 1 - y),
              jnp.where(stage == 1, y,
              jnp.where(stage == 2, 1 - y, jnp.where(second == 0, y, 1 - y))))
        row = jnp.where(stage == 0, z, jnp.where(stage == 3, zo, jnp.where(second == 0, zm, zp)))
        return col * 4 + row

    def kv_copy(kind, i):
        g = chunk_of(i)
        quad = [x, x, x, (x + 3) % 4, (x + 2) % 4][kind]
        device = [twin, ring[1], ring[2], twin, twin][kind]
        slot = (quad * 2 + c) * 8 + g + PAD
        return pltpu.make_async_remote_copy(
            src_ref=KV.at[slot], dst_ref=KV.at[slot], send_sem=kss.at[kind, i],
            recv_sem=krs.at[kind, i], device_id=device, device_id_type=MESH,
        )

    lane = lax.broadcasted_iota(jnp.int32, (ROWS, HD), 1)
    scale = math.log2(math.e) / math.sqrt(HD)

    def project(stage):
        ga, gb = chunk_of(2 * stage), chunk_of(2 * stage + 1)
        rows = jnp.concatenate([X[ga, :, 0:D], X[gb, :, 0:D]], axis=0)
        pair = (ga, gb)
        turns = []
        for g in pair:
            rc = b * 8 + g
            bc, bs = base_cos[pl.ds(rc, 1), :], base_sin[pl.ds(rc, 1), :]
            cosine = bc * step_cos[...] - bs * step_sin[...]
            sine = bs * step_cos[...] + bc * step_sin[...]
            turns.append((cosine, jnp.where(lane < 64, -sine, sine)))
        kv = dot(rows, WKV[...])
        for k, g in enumerate(pair):
            cosine, sine = turns[k]
            slot = b * 8 + g + PAD
            key = kv[k * ROWS : (k + 1) * ROWS, 0:HD]
            key = key * cosine + pltpu.roll(key, 64, 1) * sine
            KV[slot, 0:HD, :] = key.T.astype(BF16)
            KV[slot, HD:KROWS, :] = X[g, 0:FEATS, D : D + ROWS]
            KV[slot, KROWS : KROWS + HD, :] = kv[k * ROWS : (k + 1) * ROWS, HD : 2 * HD].astype(BF16)
        for i in (0, 1):
            for kind in range(3):
                kv_copy(kind, 2 * stage + i).start()
        for n in range(2):
            part = dot(rows, WQ[:, n * 256 : (n + 1) * 256])
            for k, g in enumerate(pair):
                cosine, sine = turns[k]
                for m in range(2):
                    head = part[k * ROWS : (k + 1) * ROWS, m * HD : (m + 1) * HD]
                    head = (head * cosine + pltpu.roll(head, 64, 1) * sine) * scale
                    for half in range(2):
                        at = half * 256 + (n * 2 + m) * 64
                        QE[g, at : at + 64, 0:HD] = head[half * 64 : half * 64 + 64].astype(BF16)
        for g in pair:
            mine = X[g, :, D : D + ROWS].astype(F32).T
            ext = jnp.where(lane < 8, jnp.where(mine > 0.5, 0.0, -BIG), jnp.where(lane == 8, -BIG, 0.0))
            for m in range(8):
                at = (m // 4) * 64
                QE[g, m * 64 : m * 64 + 64, HD : 2 * HD] = ext[at : at + 64].astype(BF16)

    def forward_kv(stage):
        for i in (0, 1):
            for kind in (1, 2):
                kv_copy(kind, 2 * stage + i).wait_recv()
                kv_copy(kind + 2, 2 * stage + i).start()

    for load in loads[:3]:
        load.wait()

    pick_row = lax.broadcasted_iota(jnp.int32, (128, 512), 0)
    pick_col = lax.broadcasted_iota(jnp.int32, (128, 512), 1)
    chosen = (pick_col == (pick_row // 32) * 128 + z * 32 + pick_row % 32)
    chosen = jnp.where(chosen, 1.0, 0.0).astype(BF16)

    def gram_rows(last):
        slabs = [chunk_of(i) for i in ((6, 7) if last else range(6))]
        count = len(slabs) * ROWS
        for group in range(4):
            parts = []
            for n in range(4):
                q = (n % 2) * 8 + (2 * (group % 2) + n // 2) * 2 + group // 2
                at = pl.ds(pl.multiple_of(q * 256 + y * 128, 128), 128)
                parts.append(jnp.concatenate([X[g, :, at] for g in slabs], axis=0))
            taken = jnp.concatenate(parts, axis=1)
            picked = dot(chosen, taken, (((1,), (1,)), ((), ())))
            PKT[group * 128 : (group + 1) * 128, 0:count] = picked.astype(BF16)

        def gram_tile(n, _):
            at = pl.ds(pl.multiple_of(n * 256, 256), 256)
            tile = dot(PKT[:, 0:count], jnp.concatenate([X[g, :, at] for g in slabs], axis=0))
            if last:
                GP[0, :, at] = (tile[0:256] + S0[:, at]).astype(BF16)
                GP[1, :, at] = (tile[256:512] + S1[:, at]).astype(BF16)
            else:
                S0[:, at] = tile[0:256]
                S1[:, at] = tile[256:512]
            return 0

        lax.fori_loop(0, 16, gram_tile, 0)

    def gather_stage(stage, _):
        @pl.when(stage == 0)
        def _():
            for k in (0, 1):
                z_last[k].wait_recv()
                half_last[k].start()
                y_near[k].start()
            y_first.wait_recv()
            for k in (0, 1):
                n_first[k].start()
            for k in (0, 1):
                z_first[k].wait_recv()
                half_first[k].start()
            y_last.wait_recv()

        @pl.when(stage == 1)
        def _():
            for k in (0, 1):
                half_last[k].wait_recv()
                y_oppo[k].start()

        @pl.when(stage == 2)
        def _():
            for k in (0, 1):
                n_first[k].wait_recv()
                half_next[k].start()
            for copy in y_near:
                copy.wait_recv()

        @pl.when(stage == 3)
        def _():
            gram_rows(False)
            for copy in (*half_first, *half_next, *y_oppo):
                copy.wait_recv()

        project(stage)

        @pl.when(stage > 0)
        def _():
            forward_kv(stage - 1)

        return 0

    lax.fori_loop(0, 4, gather_stage, 0)

    wo_far.wait_recv()
    wo_twin.start()
    gram_rows(True)
    gram_twin = send(20, GP.at[1 - c], GC, twin)
    gram_twin.start()
    gram_ring = [None] + [
        send(20 + k, GP.at[c, pl.ds(pl.multiple_of(((x + k) % 4) * 64, 64), 64)], GX.at[k - 1], ring[k])
        for k in (1, 2, 3)
    ]
    gram_other = send(24, GC.at[pl.ds(pl.multiple_of((1 - a) * 32, 32), 32)], GD, other)

    forward_kv(3)

    def settle(i, _):
        kv_copy(0, i).wait_recv()
        kv_copy(3, i).wait_recv()
        kv_copy(4, i).wait_recv()
        return 0

    lax.fori_loop(0, 8, settle, 0)
    wo_twin.wait_recv()
    loads[3].wait()

    late = lax.broadcasted_iota(jnp.int32, (256, HD), 0) % 64 - lax.broadcasted_iota(jnp.int32, (256, HD), 1)
    blank = jnp.zeros((256 - KROWS, HD), BF16)
    ones = jnp.ones((HD, HD), BF16)
    steps = jnp.minimum(4, b + 1)

    def rows_of(half):
        return pl.ds(pl.multiple_of(half * 256, 256), 256)

    def keys_of(slot):
        return jnp.concatenate([KV[slot, 0:KROWS, :], blank], axis=0)

    def values_of(slot):
        return jnp.concatenate([KV[slot, KROWS : KROWS + HD, :], ones], axis=1)

    def score_first(g, half, S, MX):
        scores = jnp.where(late + half * 64 >= 0, dot(QE[g, rows_of(half), :], keys_of(b * 8 + g + PAD)), -BIG)
        S[:, WINDOW : WINDOW + HD] = scores
        MX[...] = scores

    def score_step(g, half, S, MX, t):
        first = b * 8 + g + PAD - 8 * (t + 1)
        keys = jnp.concatenate([keys_of(first + j) for j in range(8)], axis=1)
        scores = dot(QE[g, rows_of(half), :], keys)
        S[:, pl.ds(pl.multiple_of(t * 1024, 1024), 1024)] = scores
        top = MX[...]
        for j in range(8):
            top = jnp.maximum(top, scores[:, j * HD : (j + 1) * HD])
        MX[...] = top

    def mix_first(g, S, MX):
        top = jnp.max(MX[...], axis=1, keepdims=True)
        TOP[...] = jnp.broadcast_to(top, (256, HD))
        probs = jnp.exp2(S[:, WINDOW : WINDOW + HD] - TOP[...]).astype(BF16)
        ACC[...] = dot(probs, values_of(b * 8 + g + PAD))

    def mix_step(g, S, t):
        first = b * 8 + g + PAD - 8 * (t + 1)
        values = jnp.concatenate([values_of(first + j) for j in range(8)], axis=0)
        scores = S[:, pl.ds(pl.multiple_of(t * 1024, 1024), 1024)]
        top = TOP[...]
        probs = jnp.concatenate(
            [jnp.exp2(scores[:, j * HD : (j + 1) * HD] - top).astype(BF16) for j in range(8)], axis=1)
        ACC[...] += dot(probs, values)

    def mix_last(g, half):
        mixed = (ACC[:, 0:HD] / ACC[:, HD : 2 * HD]).astype(BF16)
        rows = pl.ds(pl.multiple_of(half * 64, 64), 64)
        for m in range(4):
            AT[g, rows, m * HD : (m + 1) * HD] = mixed[m * 64 : m * 64 + 64]

    def both(g, half, S, MX, next_g, next_half, next_S, next_MX):
        mix_first(g, S, MX)
        score_first(next_g, next_half, next_S, next_MX)

        def step(t, _):
            score_step(next_g, next_half, next_S, next_MX, t)
            mix_step(g, S, t)
            return 0

        lax.fori_loop(0, steps, step, 0)
        mix_last(g, half)

    top, low = pl.ds(0, 64), pl.ds(64, 64)
    turned = [
        send(25, PT.at[0, top], RA.at[0], up),
        send(26, PT.at[0, low], RA.at[1], down),
        send(27, PT.at[1, top], RF.at[0, low], up),
        send(28, PT.at[1, low], RF.at[1, top], down),
        send(29, PT.at[2, top], RF.at[0, top], up),
        send(30, PT.at[2, low], RF.at[1, low], down),
    ]

    def part_of(k, second):
        row = jnp.where(k == 0, zo, jnp.where(k == 3, z, jnp.where(second == 0, zp, zm)))
        half = jnp.where(k == 1, 1 - second, second)
        return row, half

    def swap(k, second):
        row, half = part_of(k, second)
        rows = pl.ds(pl.multiple_of(half * 64, 64), 64)
        to = pl.ds(pl.multiple_of(second * 64, 64), 64)
        return pltpu.make_async_remote_copy(
            src_ref=AT.at[(1 - y) * 4 + row, rows], dst_ref=AR.at[k, to], send_sem=sws.at[k, second],
            recv_sem=swr.at[k, second], device_id=side, device_id_type=MESH,
        )

    def out_stage(k, _):
        rows = [part_of(k, 0), part_of(k, 1)]

        def unit(i, _):
            col = jnp.where(i == 0, 1 - y, y) * 4
            after = jnp.minimum(2 * k + i + 1, 7)
            after_col = jnp.where(after % 2 == 0, 1 - y, y) * 4
            after_row, after_half = part_of(after // 2, 0)
            both(col + rows[0][0], rows[0][1], S0, M0, col + rows[1][0], rows[1][1], S1, M1)

            @pl.when(i == 0)
            def _():
                swap(k, 0).start()

            both(col + rows[1][0], rows[1][1], S1, M1, after_col + after_row, after_half, S0, M0)

            @pl.when(i == 0)
            def _():
                swap(k, 1).start()

            return 0

        lax.fori_loop(0, 2, unit, 0)
        swap(k, 0).wait_recv()
        swap(k, 1).wait_recv()
        own = jnp.concatenate(
            [AT[y * 4 + row, pl.ds(pl.multiple_of(half * 64, 64), 64), :] for row, half in rows], axis=0)

        def out_tile(n, _):
            at = pl.ds(pl.multiple_of(n * 512, 512), 512)
            PT[k, :, at] = (dot(own, WO[0, :, at]) + dot(AR[k], WO[1, :, at])).astype(BF16)
            return 0

        lax.fori_loop(0, 8, out_tile, 0)

        @pl.when(k == 0)
        def _():
            turned[0].start()
            turned[1].start()
            gram_twin.wait_recv()

            def add(n, _):
                at = pl.ds(pl.multiple_of(n * 512, 512), 512)
                GP[c, :, at] = (GP[c, :, at].astype(F32) + GC[:, at].astype(F32)).astype(BF16)
                return 0

            lax.fori_loop(0, 8, add, 0)
            for k in (1, 2, 3):
                gram_ring[k].start()

        @pl.when(k == 1)
        def _():
            turned[2].start()
            turned[3].start()

        @pl.when(k == 2)
        def _():
            for which in (0, 1):
                turned[which].wait_recv()
                at = pl.ds(64 * which, 64)
                PT[2, at] = (PT[2, at].astype(F32) + RA[which].astype(F32)).astype(BF16)
                turned[4 + which].start()

        @pl.when(k == 2)
        def _():
            for k in (1, 2, 3):
                gram_ring[k].wait_recv()

            def add(n, _):
                at = pl.ds(pl.multiple_of(n * 512, 512), 512)
                total = GP[c, pl.ds(pl.multiple_of(x * 64, 64), 64), at].astype(F32)
                for k in range(3):
                    total = total + GX[k, :, at].astype(F32)
                GC[0:64, at] = total.astype(BF16)
                return 0

            lax.fori_loop(0, 8, add, 0)
            gram_other.start()

        return 0

    start_g = (1 - y) * 4 + zo
    score_first(start_g, 0, S0, M0)

    def start_step(t, _):
        score_step(start_g, 0, S0, M0, t)
        return 0

    lax.fori_loop(0, steps, start_step, 0)
    lax.fori_loop(0, 4, out_stage, 0)
    gram_other.wait_recv()
    mine = pl.ds(pl.multiple_of(a * 32, 32), 32)
    gram[...] = GC[mine, :].astype(F32) + GD[...].astype(F32)
    for copy in turned[2:]:
        copy.wait_recv()
    out[...] = PT[3].astype(F32) + RF[0].astype(F32) + RF[1].astype(F32)

    for copy in [*gathers, wo_far, wo_twin, gram_twin,
                 *gram_ring[1:], gram_other, *turned]:
        copy.wait_send()

    def drain(i, _):
        for kind in range(5):
            kv_copy(kind, i).wait_send()
        return 0

    lax.fori_loop(0, 8, drain, 0)

    def drain_swap(k, _):
        swap(k, 0).wait_send()
        swap(k, 1).wait_send()
        return 0

    lax.fori_loop(0, 4, drain_swap, 0)


def per_device(tokens, norm_gain, segment_ids, w_query, w_key, w_value, w_out):
    vmem = pl.BlockSpec(memory_space=pltpu.VMEM)
    hbm = pl.BlockSpec(memory_space=pl.ANY)
    dma = pltpu.SemaphoreType.DMA
    scratch = [
        pltpu.VMEM((8, ROWS, D + ROWS), BF16),
        pltpu.VMEM((D, 512), BF16),
        pltpu.VMEM((D, 256), BF16),
        pltpu.VMEM((2, 512, D), BF16),
        pltpu.VMEM((8, 512, 256), BF16),
        pltpu.VMEM((64 + PAD, KROWS + HD, HD), BF16),
        pltpu.VMEM((512, 768), BF16),
        pltpu.VMEM((2, 256, D), BF16),
        pltpu.VMEM((256, D), BF16),
        pltpu.VMEM((3, 64, D), BF16),
        pltpu.VMEM((32, D), BF16),
        pltpu.VMEM((8, ROWS, 512), BF16),
        pltpu.VMEM((4, ROWS, 512), BF16),
        pltpu.VMEM((4, ROWS, D), BF16),
        pltpu.VMEM((2, 64, D), BF16),
        pltpu.VMEM((2, ROWS, D), BF16),
        pltpu.VMEM((256, 256), F32),
        pltpu.VMEM((256, HD), F32),
        pltpu.VMEM((256, WINDOW + HD), F32),
        pltpu.VMEM((256, WINDOW + HD), F32),
        pltpu.VMEM((256, HD), F32),
        pltpu.VMEM((256, HD), F32),
        dma((40,)),
        dma((40,)),
        dma((5, 8)),
        dma((5, 8)),
        dma((4, 2)),
        dma((4, 2)),
        dma((4,)),
    ]
    delta, gram = pl.pallas_call(
        kernel,
        out_shape=(jax.ShapeDtypeStruct((ROWS, D), F32), jax.ShapeDtypeStruct((32, D), F32)),
        in_specs=[vmem, vmem, vmem, hbm, hbm, hbm, hbm, vmem, vmem, vmem, vmem],
        out_specs=(vmem, vmem),
        scratch_shapes=scratch,
        compiler_params=pltpu.CompilerParams(
            collective_id=0, has_side_effects=True, vmem_limit_bytes=62 << 20),
        name="sublayer",
    )(tokens[0], norm_gain[None], segment_ids, w_query, w_key, w_value, w_out,
      *[jnp.asarray(t) for t in tables()])
    return delta.astype(BF16)[None], gram * (1.0 / 16384.0)


def solution(mesh):
    return jax.shard_map(
        per_device,
        mesh=mesh,
        in_specs=(
            P("dp", ("blk", "heads"), None),
            P(),
            P("dp", ("blk", "heads")),
            P(None, "heads"),
            P(None, "heads"),
            P(None, "heads"),
            P("heads", None),
        ),
        out_specs=(P("dp", ("blk", "heads"), None), P(("dp", "blk", "heads"), None)),
        check_vma=False,
    )
```

```python
import math

import jax
import jax.numpy as jnp
import numpy as np
from jax import lax
from jax.experimental import pallas as pl
from jax.experimental.pallas import tpu as pltpu
from jax.sharding import PartitionSpec as P

MESH = pl.DeviceIdType.MESH
HD = 128
D = 4096
ROWS = 128
EPSILON = 1e-05
ROPE_BASE = 500000.0
BIG = 1e30
FEATS = 16
KROWS = HD + FEATS
SPAN = 16
OUT = 4096
TILE = 1024
PAD = SPAN
CUT = 18 * 128
WINDOW = 4096
F32 = jnp.float32
BF16 = jnp.bfloat16


def tables():
    frequency = ROPE_BASE ** (-(np.arange(64, dtype=np.float64) * 2.0 / HD))
    frequency = np.concatenate([frequency, frequency])
    base = np.arange(64)[:, None] * float(ROWS) * frequency[None, :]
    step = np.arange(ROWS)[:, None] * frequency[None, :]
    return [f(v).astype(np.float32) for v in (base, step) for f in (np.cos, np.sin)]


def dot(a, b, dims=(((1,), (0,)), ((), ()))):
    return lax.dot_general(a, b, dims, preferred_element_type=F32)


def kernel(
    tok, gain, seg, wq_h, wk_h, wv_h, wo_h, base_cos, base_sin, step_cos, step_sin,
    out, gram,
    X, WQ, WKV, WO, QE, KV, PKT, GP, GC, GX, GT, GD, AT, AR, PT, RA, RF, ACC, TOP, S0, S1, M0, M1,
    ss, rs, kss, krs, sws, swr, gss, grs, ls,
):
    a, b, h = lax.axis_index("dp"), lax.axis_index("blk"), lax.axis_index("heads")
    x, c = b // 2, b % 2
    y, z = h // 4, h % 4
    zp, zm, zo = (z + 1) % 4, (z + 3) % 4, (z + 2) % 4
    up, down = (a, b, y * 4 + zp), (a, b, y * 4 + zm)
    side = (a, b, (1 - y) * 4 + z)
    far = (1 - a, b, (1 - y) * 4 + z)
    twin = (a, x * 2 + 1 - c, h)
    other = (1 - a, b, h)
    ring = [None] + [(a, ((x + k) % 4) * 2 + c, h) for k in (1, 2, 3)]

    loads = [
        pltpu.make_async_copy(wk_h, WKV.at[:, 0:HD], ls.at[0]),
        pltpu.make_async_copy(wv_h, WKV.at[:, HD : 2 * HD], ls.at[1]),
        pltpu.make_async_copy(wq_h, WQ, ls.at[2]),
        pltpu.make_async_copy(wo_h, WO.at[0], ls.at[3]),
    ]
    for load in loads:
        load.start()

    barrier = pltpu.get_barrier_semaphore()
    partners = [up, down, side, far, twin, other] + ring[1:]
    for partner in partners:
        pl.semaphore_signal(barrier, inc=1, device_id=partner, device_id_type=MESH)

    def normalise(i, _):
        at = pl.ds(pl.multiple_of(i * 16, 16), 16)
        values = tok[at, :].astype(F32)
        mean_square = jnp.mean(values * values, axis=-1, keepdims=True)
        X[h, at, 0:D] = (values * lax.rsqrt(mean_square + EPSILON) * gain[...]).astype(BF16)
        return 0

    lax.fori_loop(0, ROWS // 16, normalise, 0)
    feature = lax.broadcasted_iota(jnp.int32, (ROWS, ROWS), 0)
    X[h, :, D : D + ROWS] = jnp.where(feature == seg[...], 1.0, 0.0).astype(BF16)

    pl.semaphore_wait(barrier, len(partners))

    def send(i, src, dst, device):
        return pltpu.make_async_remote_copy(
            src_ref=src, dst_ref=dst, send_sem=ss.at[i], recv_sem=rs.at[i],
            device_id=device, device_id_type=MESH,
        )

    FIRST, LAST = pl.ds(0, CUT), pl.ds(CUT, D + ROWS - CUT)

    def move(i, g, columns, device, half=None):
        rows = pl.ds(0, ROWS) if half is None else pl.ds(half * 64, 64)
        return send(i, X.at[g, rows, columns], X.at[g, rows, columns], device)

    hs = (1 - y) * 4 + z
    om, op, oo = y * 4 + zm, y * 4 + zp, y * 4 + zo
    nm, np_ = (1 - y) * 4 + zm, (1 - y) * 4 + zp
    y_first = move(0, h, FIRST, side)
    y_last = move(1, h, LAST, side)
    z_first = [move(2, h, FIRST, up), move(3, h, FIRST, down)]
    z_last = [move(4, h, LAST, up), move(5, h, LAST, down)]
    n_first = [move(6, hs, FIRST, up), move(7, hs, FIRST, down)]
    half_first = [move(8, om, FIRST, up, 0), move(9, op, FIRST, down, 1)]
    half_last = [move(10, om, LAST, up, 0), move(11, op, LAST, down, 1)]
    y_near = [move(12, om, LAST, side), move(13, op, LAST, side)]
    y_oppo = [move(14, oo, LAST, side, 0), move(15, oo, LAST, side, 1)]
    half_next = [move(16, nm, FIRST, up, 0), move(17, np_, FIRST, down, 1)]
    gathers = [y_first, y_last, *z_first, *z_last, *n_first, *half_first, *half_last, *y_near, *y_oppo, *half_next]
    for copy in (y_first, *z_last, *z_first, y_last):
        copy.start()
    half_rows = pl.ds(pl.multiple_of(c * 256, 256), 256)
    wo_far = send(18, wo_h.at[half_rows], WO.at[1, half_rows], far)
    wo_far.start()
    wo_twin = send(19, WO.at[1, half_rows], WO.at[1, half_rows], twin)

    pads = lax.broadcasted_iota(jnp.int32, (FEATS, HD), 0)
    def clear(slot, _):
        KV[slot] = jnp.zeros((KROWS + HD, HD), BF16)
        KV[slot, HD:KROWS, :] = jnp.where(pads == 8, 1.0, 0.0).astype(BF16)
        return 0

    lax.fori_loop(0, PAD, clear, 0)

    def chunk_of(i):
        stage, second = i // 2, i % 2
        col = jnp.where(stage == 0, jnp.where(second == 0, y, 1 - y),
              jnp.where(stage == 1, y,
              jnp.where(stage == 2, 1 - y, jnp.where(second == 0, y, 1 - y))))
        row = jnp.where(stage == 0, z, jnp.where(stage == 3, zo, jnp.where(second == 0, zm, zp)))
        return col * 4 + row

    def kv_copy(kind, i):
        g = chunk_of(i)
        quad = [x, x, x, (x + 3) % 4, (x + 2) % 4][kind]
        device = [twin, ring[1], ring[2], twin, twin][kind]
        slot = (quad * 2 + c) * 8 + g + PAD
        return pltpu.make_async_remote_copy(
            src_ref=KV.at[slot], dst_ref=KV.at[slot], send_sem=kss.at[kind, i],
            recv_sem=krs.at[kind, i], device_id=device, device_id_type=MESH,
        )

    lane = lax.broadcasted_iota(jnp.int32, (ROWS, HD), 1)
    scale = math.log2(math.e) / math.sqrt(HD)

    def project(items):
        pair = [chunk_of(i) for i in items]
        rows = jnp.concatenate([X[g, :, 0:D] for g in pair], axis=0)
        turns = []
        for g in pair:
            rc = b * 8 + g
            bc, bs = base_cos[pl.ds(rc, 1), :], base_sin[pl.ds(rc, 1), :]
            cosine = bc * step_cos[...] - bs * step_sin[...]
            sine = bs * step_cos[...] + bc * step_sin[...]
            turns.append((cosine, jnp.where(lane < 64, -sine, sine)))
        kv = dot(rows, WKV[...])
        for k, g in enumerate(pair):
            cosine, sine = turns[k]
            slot = b * 8 + g + PAD
            key = kv[k * ROWS : (k + 1) * ROWS, 0:HD]
            key = key * cosine + pltpu.roll(key, 64, 1) * sine
            KV[slot, 0:HD, :] = key.T.astype(BF16)
            KV[slot, HD:KROWS, :] = X[g, 0:FEATS, D : D + ROWS]
            KV[slot, KROWS : KROWS + HD, :] = kv[k * ROWS : (k + 1) * ROWS, HD : 2 * HD].astype(BF16)
        for i in items:
            for kind in range(3):
                kv_copy(kind, i).start()
        for n in range(2):
            part = dot(rows, WQ[:, n * 256 : (n + 1) * 256])
            for k, g in enumerate(pair):
                cosine, sine = turns[k]
                for m in range(2):
                    head = part[k * ROWS : (k + 1) * ROWS, m * HD : (m + 1) * HD]
                    head = (head * cosine + pltpu.roll(head, 64, 1) * sine) * scale
                    for half in range(2):
                        at = half * 256 + (n * 2 + m) * 64
                        QE[g, at : at + 64, 0:HD] = head[half * 64 : half * 64 + 64].astype(BF16)
        for g in pair:
            mine = X[g, :, D : D + ROWS].astype(F32).T
            ext = jnp.where(lane < 8, jnp.where(mine > 0.5, 0.0, -BIG), jnp.where(lane == 8, -BIG, 0.0))
            for m in range(8):
                at = (m // 4) * 64
                QE[g, m * 64 : m * 64 + 64, HD : 2 * HD] = ext[at : at + 64].astype(BF16)

    def forward_kv(items):
        for i in items:
            for kind in (1, 2):
                kv_copy(kind, i).wait_recv()
                kv_copy(kind + 2, i).start()

    for load in loads[:3]:
        load.wait()

    pick_row = lax.broadcasted_iota(jnp.int32, (128, 512), 0)
    pick_col = lax.broadcasted_iota(jnp.int32, (128, 512), 1)
    chosen = (pick_col == (pick_row // 32) * 128 + z * 32 + pick_row % 32)
    chosen = jnp.where(chosen, 1.0, 0.0).astype(BF16)

    def tile_copy(kind, n, src, dst, device):
        return pltpu.make_async_remote_copy(
            src_ref=src, dst_ref=dst, send_sem=gss.at[kind, n], recv_sem=grs.at[kind, n],
            device_id=device, device_id_type=MESH,
        )

    def tile_at(n):
        return pl.ds(pl.multiple_of(n * TILE, TILE), TILE)

    def gram_twin(n):
        return tile_copy(0, n, GP.at[1 - c, :, tile_at(n)], GC.at[:, tile_at(n)], twin)

    def gram_ring(n):
        return [tile_copy(k, n, GP.at[c, pl.ds(pl.multiple_of(((x + k) % 4) * 64, 64), 64), tile_at(n)],
                          GX.at[k - 1, :, tile_at(n)], ring[k]) for k in (1, 2, 3)]

    def gram_other(n):
        rows = pl.ds(pl.multiple_of((1 - a) * 32, 32), 32)
        return tile_copy(4, n, GT.at[rows, tile_at(n)], GD.at[:, tile_at(n)], other)

    def gram_rows(last):
        slabs = [chunk_of(i) for i in ((6, 7) if last else range(6))]
        count = len(slabs) * ROWS
        for group in range(4):
            parts = []
            for n in range(4):
                q = (n % 2) * 8 + (2 * (group % 2) + n // 2) * 2 + group // 2
                at = pl.ds(pl.multiple_of(q * 256 + y * 128, 128), 128)
                parts.append(jnp.concatenate([X[g, :, at] for g in slabs], axis=0))
            taken = jnp.concatenate(parts, axis=1)
            picked = dot(chosen, taken, (((1,), (1,)), ((), ())))
            PKT[group * 128 : (group + 1) * 128, 0:count] = picked.astype(BF16)

        def gram_tile(n, _):
            at = pl.ds(pl.multiple_of(n * TILE, TILE), TILE)
            tile = dot(PKT[:, 0:count], jnp.concatenate([X[g, :, at] for g in slabs], axis=0))
            if last:
                GP[0, :, at] = (tile[0:256] + S0[:, at]).astype(BF16)
                GP[1, :, at] = (tile[256:512] + S1[:, at]).astype(BF16)
                gram_twin(n).start()
            else:
                S0[:, at] = tile[0:256]
                S1[:, at] = tile[256:512]
            return 0

        lax.fori_loop(0, D // TILE, gram_tile, 0)

    def gather_stage(stage, _):
        @pl.when(stage == 0)
        def _():
            for k in (0, 1):
                z_last[k].wait_recv()
                half_last[k].start()
                y_near[k].start()
            y_first.wait_recv()
            for k in (0, 1):
                n_first[k].start()
            for k in (0, 1):
                z_first[k].wait_recv()
                half_first[k].start()
            y_last.wait_recv()

        @pl.when(stage == 1)
        def _():
            for k in (0, 1):
                half_last[k].wait_recv()
                y_oppo[k].start()

        @pl.when(stage == 2)
        def _():
            for k in (0, 1):
                n_first[k].wait_recv()
                half_next[k].start()
            for copy in y_near:
                copy.wait_recv()

        project((2 * stage, 2 * stage + 1))

        @pl.when(stage > 0)
        def _():
            forward_kv((2 * stage - 2, 2 * stage - 1))

        return 0

    lax.fori_loop(0, 3, gather_stage, 0)
    gram_rows(False)
    forward_kv((4, 5))

    def gather_last(i, _):
        @pl.when(i == 0)
        def _():
            for copy in half_first:
                copy.wait_recv()

        @pl.when(i == 1)
        def _():
            for copy in (*half_next, *y_oppo):
                copy.wait_recv()

        project((6 + i,))
        return 0

    lax.fori_loop(0, 2, gather_last, 0)
    forward_kv((6,))

    wo_far.wait_recv()
    wo_twin.start()
    gram_rows(True)
    forward_kv((7,))

    def settle(i, _):
        kv_copy(0, i).wait_recv()
        kv_copy(3, i).wait_recv()
        kv_copy(4, i).wait_recv()
        return 0

    lax.fori_loop(0, 8, settle, 0)
    wo_twin.wait_recv()
    loads[3].wait()

    late = lax.broadcasted_iota(jnp.int32, (256, HD), 0) % 64 - lax.broadcasted_iota(jnp.int32, (256, HD), 1)
    blank = jnp.zeros((256 - KROWS, HD), BF16)
    ones = jnp.ones((HD, HD), BF16)
    steps = jnp.minimum(32 // SPAN, (8 * b + 7 + SPAN) // SPAN)

    def rows_of(half):
        return pl.ds(pl.multiple_of(half * 256, 256), 256)

    def keys_of(slot):
        return jnp.concatenate([KV[slot, 0:KROWS, :], blank], axis=0)

    def values_of(slot):
        return jnp.concatenate([KV[slot, KROWS : KROWS + HD, :], ones], axis=1)

    def score_first(g, half, S, MX):
        scores = jnp.where(late + half * 64 >= 0, dot(QE[g, rows_of(half), :], keys_of(b * 8 + g + PAD)), -BIG)
        S[:, WINDOW : WINDOW + HD] = scores
        MX[...] = scores

    def score_step(g, half, S, MX, t):
        first = b * 8 + g + PAD - SPAN * (t + 1)
        keys = jnp.concatenate([keys_of(first + j) for j in range(SPAN)], axis=1)
        scores = dot(QE[g, rows_of(half), :], keys)
        S[:, pl.ds(pl.multiple_of(t * SPAN * HD, SPAN * HD), SPAN * HD)] = scores
        top = MX[...]
        for j in range(SPAN):
            top = jnp.maximum(top, scores[:, j * HD : (j + 1) * HD])
        MX[...] = top

    def mix_first(g, S, MX):
        top = jnp.max(MX[...], axis=1, keepdims=True)
        TOP[...] = jnp.broadcast_to(top, (256, HD))
        probs = jnp.exp2(S[:, WINDOW : WINDOW + HD] - TOP[...]).astype(BF16)
        ACC[...] = dot(probs, values_of(b * 8 + g + PAD))

    def mix_step(g, S, t):
        first = b * 8 + g + PAD - SPAN * (t + 1)
        values = jnp.concatenate([values_of(first + j) for j in range(SPAN)], axis=0)
        scores = S[:, pl.ds(pl.multiple_of(t * SPAN * HD, SPAN * HD), SPAN * HD)]
        top = TOP[...]
        probs = jnp.concatenate(
            [jnp.exp2(scores[:, j * HD : (j + 1) * HD] - top).astype(BF16) for j in range(SPAN)], axis=1)
        ACC[...] += dot(probs, values)

    def mix_last(g, half):
        mixed = (ACC[:, 0:HD] / ACC[:, HD : 2 * HD]).astype(BF16)
        rows = pl.ds(pl.multiple_of(half * 64, 64), 64)
        for m in range(4):
            AT[g, rows, m * HD : (m + 1) * HD] = mixed[m * 64 : m * 64 + 64]

    def both(g, half, S, MX, next_g, next_half, next_S, next_MX):
        mix_first(g, S, MX)
        score_first(next_g, next_half, next_S, next_MX)

        def step(t, _):
            score_step(next_g, next_half, next_S, next_MX, t)
            mix_step(g, S, t)
            return 0

        lax.fori_loop(0, steps, step, 0)
        mix_last(g, half)

    top, low = pl.ds(0, 64), pl.ds(64, 64)
    turned = [
        send(25, PT.at[0, top], RA.at[0], up),
        send(26, PT.at[0, low], RA.at[1], down),
        send(27, PT.at[1, top], RF.at[0, low], up),
        send(28, PT.at[1, low], RF.at[1, top], down),
        send(29, PT.at[2, top], RF.at[0, top], up),
        send(30, PT.at[2, low], RF.at[1, low], down),
    ]

    def part_of(k, second):
        row = jnp.where(k == 0, zo, jnp.where(k == 3, z, jnp.where(second == 0, zp, zm)))
        half = jnp.where(k == 1, 1 - second, second)
        return row, half

    def swap(k, second):
        row, half = part_of(k, second)
        rows = pl.ds(pl.multiple_of(half * 64, 64), 64)
        to = pl.ds(pl.multiple_of(second * 64, 64), 64)
        return pltpu.make_async_remote_copy(
            src_ref=AT.at[(1 - y) * 4 + row, rows], dst_ref=AR.at[k, to], send_sem=sws.at[k, second],
            recv_sem=swr.at[k, second], device_id=side, device_id_type=MESH,
        )

    def gram_cores():
        def add(n, _):
            gram_twin(n).wait_recv()
            at = tile_at(n)
            GP[c, :, at] = (GP[c, :, at].astype(F32) + GC[:, at].astype(F32)).astype(BF16)
            for copy in gram_ring(n):
                copy.start()
            return 0

        lax.fori_loop(0, D // TILE, add, 0)

    def gram_quads(n):
        for copy in gram_ring(n):
            copy.wait_recv()
        at = tile_at(n)
        total = GP[c, pl.ds(pl.multiple_of(x * 64, 64), 64), at].astype(F32)
        for i in range(3):
            total = total + GX[i, :, at].astype(F32)
        GT[:, at] = total.astype(BF16)
        gram_other(n).start()

    def out_stage(k, _):
        rows = [part_of(k, 0), part_of(k, 1)]

        def unit(i, _):
            col = jnp.where(i == 0, 1 - y, y) * 4
            after = jnp.minimum(2 * k + i + 1, 7)
            after_col = jnp.where(after % 2 == 0, 1 - y, y) * 4
            after_row, after_half = part_of(after // 2, 0)
            both(col + rows[0][0], rows[0][1], S0, M0, col + rows[1][0], rows[1][1], S1, M1)

            @pl.when(i == 0)
            def _():
                swap(k, 0).start()

            both(col + rows[1][0], rows[1][1], S1, M1, after_col + after_row, after_half, S0, M0)

            @pl.when(i == 0)
            def _():
                swap(k, 1).start()

            @pl.when((i == 0) & (k == 0))
            def _():
                gram_cores()

            @pl.when((k == 1) | (k == 2))
            def _():
                gram_quads(2 * k - 2 + i)

            return 0

        lax.fori_loop(0, 2, unit, 0)
        swap(k, 0).wait_recv()
        swap(k, 1).wait_recv()
        own = jnp.concatenate(
            [AT[y * 4 + row, pl.ds(pl.multiple_of(half * 64, 64), 64), :] for row, half in rows], axis=0)

        def out_tile(n, _):
            at = pl.ds(pl.multiple_of(n * OUT, OUT), OUT)
            PT[k, :, at] = (dot(own, WO[0, :, at]) + dot(AR[k], WO[1, :, at])).astype(BF16)
            return 0

        lax.fori_loop(0, D // OUT, out_tile, 0)

        @pl.when(k == 0)
        def _():
            turned[0].start()
            turned[1].start()

        @pl.when(k == 1)
        def _():
            turned[2].start()
            turned[3].start()

        @pl.when(k == 2)
        def _():
            for which in (0, 1):
                turned[which].wait_recv()
                at = pl.ds(64 * which, 64)
                PT[2, at] = (PT[2, at].astype(F32) + RA[which].astype(F32)).astype(BF16)
                turned[4 + which].start()

        return 0

    start_g = (1 - y) * 4 + zo
    score_first(start_g, 0, S0, M0)

    def start_step(t, _):
        score_step(start_g, 0, S0, M0, t)
        return 0

    lax.fori_loop(0, steps, start_step, 0)
    lax.fori_loop(0, 4, out_stage, 0)
    mine = pl.ds(pl.multiple_of(a * 32, 32), 32)
    for n in range(D // TILE):
        gram_other(n).wait_recv()
    gram[...] = GT[mine, :].astype(F32) + GD[...].astype(F32)
    for copy in turned[2:]:
        copy.wait_recv()
    out[...] = (PT[3].astype(F32) + RF[0].astype(F32) + RF[1].astype(F32)).astype(BF16)

    for copy in [*gathers, wo_far, wo_twin, *turned]:
        copy.wait_send()

    def drain(i, _):
        for kind in range(5):
            kv_copy(kind, i).wait_send()
        return 0

    lax.fori_loop(0, 8, drain, 0)

    def drain_gram(n, _):
        for copy in (gram_twin(n), *gram_ring(n), gram_other(n)):
            copy.wait_send()
        return 0

    lax.fori_loop(0, D // TILE, drain_gram, 0)

    def drain_swap(k, _):
        swap(k, 0).wait_send()
        swap(k, 1).wait_send()
        return 0

    lax.fori_loop(0, 4, drain_swap, 0)


def finish(delta, gram, delta_out, gram_out):
    delta_out[...] = delta[...]
    gram_out[...] = gram[...] * (1.0 / 16384.0)


def per_device(tokens, norm_gain, segment_ids, w_query, w_key, w_value, w_out):
    vmem = pl.BlockSpec(memory_space=pltpu.VMEM)
    hbm = pl.BlockSpec(memory_space=pl.ANY)
    dma = pltpu.SemaphoreType.DMA
    scratch = [
        pltpu.VMEM((8, ROWS, D + ROWS), BF16),
        pltpu.VMEM((D, 512), BF16),
        pltpu.VMEM((D, 256), BF16),
        pltpu.VMEM((2, 512, D), BF16),
        pltpu.VMEM((8, 512, 256), BF16),
        pltpu.VMEM((64 + PAD, KROWS + HD, HD), BF16),
        pltpu.VMEM((512, 768), BF16),
        pltpu.VMEM((2, 256, D), BF16),
        pltpu.VMEM((256, D), BF16),
        pltpu.VMEM((3, 64, D), BF16),
        pltpu.VMEM((64, D), BF16),
        pltpu.VMEM((32, D), BF16),
        pltpu.VMEM((8, ROWS, 512), BF16),
        pltpu.VMEM((4, ROWS, 512), BF16),
        pltpu.VMEM((4, ROWS, D), BF16),
        pltpu.VMEM((2, 64, D), BF16),
        pltpu.VMEM((2, ROWS, D), BF16),
        pltpu.VMEM((256, 256), F32),
        pltpu.VMEM((256, HD), F32),
        pltpu.VMEM((256, WINDOW + HD), F32),
        pltpu.VMEM((256, WINDOW + HD), F32),
        pltpu.VMEM((256, HD), F32),
        pltpu.VMEM((256, HD), F32),
        dma((40,)),
        dma((40,)),
        dma((5, 8)),
        dma((5, 8)),
        dma((4, 2)),
        dma((4, 2)),
        dma((5, 4)),
        dma((5, 4)),
        dma((4,)),
    ]
    delta, gram = pl.pallas_call(
        kernel,
        out_shape=(jax.ShapeDtypeStruct((ROWS, D), BF16), jax.ShapeDtypeStruct((32, D), F32)),
        in_specs=[vmem, vmem, vmem, hbm, hbm, hbm, hbm, vmem, vmem, vmem, vmem],
        out_specs=(vmem, vmem),
        scratch_shapes=scratch,
        compiler_params=pltpu.CompilerParams(
            collective_id=0, has_side_effects=True, vmem_limit_bytes=62 << 20),
        name="sublayer",
    )(tokens[0], norm_gain[None], segment_ids, w_query, w_key, w_value, w_out,
      *[jnp.asarray(t) for t in tables()])
    delta, gram = pl.pallas_call(
        finish,
        out_shape=(jax.ShapeDtypeStruct((ROWS, D), BF16), jax.ShapeDtypeStruct((32, D), F32)),
        in_specs=[vmem, vmem],
        out_specs=(vmem, vmem),
        name="finish",
    )(delta, gram)
    return delta[None], gram


def solution(mesh):
    return jax.shard_map(
        per_device,
        mesh=mesh,
        in_specs=(
            P("dp", ("blk", "heads"), None),
            P(),
            P("dp", ("blk", "heads")),
            P(None, "heads"),
            P(None, "heads"),
            P(None, "heads"),
            P("heads", None),
        ),
        out_specs=(P("dp", ("blk", "heads"), None), P(("dp", "blk", "heads"), None)),
        check_vma=False,
    )
```

```python
import math

import jax
import jax.numpy as jnp
import numpy as np
from jax import lax
from jax.experimental import pallas as pl
from jax.experimental.pallas import tpu as pltpu
from jax.sharding import PartitionSpec as P

MESH = pl.DeviceIdType.MESH
HD = 128
D = 4096
ROWS = 128
EPSILON = 1e-05
ROPE_BASE = 500000.0
BIG = 1e30
FEATS = 16
KROWS = HD + FEATS
SPAN = 16
OUT = 2048
TILE = 1024
PAD = SPAN
CUT = 18 * 128
WINDOW = 4096
F32 = jnp.float32
BF16 = jnp.bfloat16


def tables():
    frequency = ROPE_BASE ** (-(np.arange(64, dtype=np.float64) * 2.0 / HD))
    frequency = np.concatenate([frequency, frequency])
    base = np.arange(64)[:, None] * float(ROWS) * frequency[None, :]
    step = np.arange(ROWS)[:, None] * frequency[None, :]
    return [f(v).astype(np.float32) for v in (base, step) for f in (np.cos, np.sin)]


def dot(a, b, dims=(((1,), (0,)), ((), ()))):
    return lax.dot_general(a, b, dims, preferred_element_type=F32)


def kernel(
    tok_h, gain, seg, wq_h, wk_h, wv_h, wo_h, base_cos, base_sin, step_cos, step_sin,
    out, gram,
    X, E, tok, WQ, WKV, WO, QE, KV, PKT, GP, GC, GX, GT, GD, AT, AR, PT, RA, RF, ACC, TOP, S0, S1, M0, M1,
    ss, rs, kss, krs, sws, swr, gss, grs, ess, ers, tss, trs, ls,
):
    a, b, h = lax.axis_index("dp"), lax.axis_index("blk"), lax.axis_index("heads")
    x, c = b // 2, b % 2
    y, z = h // 4, h % 4
    zp, zm, zo = (z + 1) % 4, (z + 3) % 4, (z + 2) % 4
    up, down = (a, b, y * 4 + zp), (a, b, y * 4 + zm)
    side = (a, b, (1 - y) * 4 + z)
    far = (1 - a, b, (1 - y) * 4 + z)
    twin = (a, x * 2 + 1 - c, h)
    other = (1 - a, b, h)
    ring = [None] + [(a, ((x + k) % 4) * 2 + c, h) for k in (1, 2, 3)]

    load_tok = pltpu.make_async_copy(tok_h, tok, ls.at[4])
    load_tok.start()
    loads = [
        pltpu.make_async_copy(wk_h, WKV.at[:, 0:HD], ls.at[0]),
        pltpu.make_async_copy(wv_h, WKV.at[:, HD : 2 * HD], ls.at[1]),
        pltpu.make_async_copy(wq_h, WQ, ls.at[2]),
        pltpu.make_async_copy(wo_h, WO.at[0], ls.at[3]),
    ]
    barrier = pltpu.get_barrier_semaphore()
    group = [(a, b, ((y + j // 4) % 2) * 4 + (z + j) % 4) for j in range(1, 8)]
    partners = group + [far, twin, other] + ring[1:]
    for partner in partners:
        pl.semaphore_signal(barrier, inc=1, device_id=partner, device_id_type=MESH)

    load_tok.wait()
    for load in loads:
        load.start()

    def normalise(i, _):
        at = pl.ds(pl.multiple_of(i * 16, 16), 16)
        values = tok[at, :].astype(F32)
        mean_square = jnp.mean(values * values, axis=-1, keepdims=True)
        X[h, at, 0:D] = (values * lax.rsqrt(mean_square + EPSILON) * gain[...]).astype(BF16)
        return 0

    lax.fori_loop(0, ROWS // 16, normalise, 0)
    feature = lax.broadcasted_iota(jnp.int32, (FEATS, ROWS), 0)
    E[h] = jnp.where(feature == seg[...], 1.0, 0.0).astype(BF16)

    pl.semaphore_wait(barrier, len(partners))

    def send(i, src, dst, device):
        return pltpu.make_async_remote_copy(
            src_ref=src, dst_ref=dst, send_sem=ss.at[i], recv_sem=rs.at[i],
            device_id=device, device_id_type=MESH,
        )

    FIRST, LAST = pl.ds(0, CUT), pl.ds(CUT, D - CUT)

    def move(i, g, columns, device, half=None):
        rows = pl.ds(0, ROWS) if half is None else pl.ds(half * 64, 64)
        return send(i, X.at[g, rows, columns], X.at[g, rows, columns], device)

    hs = (1 - y) * 4 + z
    om, op, oo = y * 4 + zm, y * 4 + zp, y * 4 + zo
    nm, np_ = (1 - y) * 4 + zm, (1 - y) * 4 + zp
    y_first = move(0, h, FIRST, side)
    y_last = move(1, h, LAST, side)
    z_first = [move(2, h, FIRST, up), move(3, h, FIRST, down)]
    z_last = [move(4, h, LAST, up), move(5, h, LAST, down)]
    n_first = [move(6, hs, FIRST, up), move(7, hs, FIRST, down)]
    half_first = [move(8, om, FIRST, up, 0), move(9, op, FIRST, down, 1)]
    half_last = [move(10, om, LAST, up, 0), move(11, op, LAST, down, 1)]
    y_near = [move(12, om, LAST, side), move(13, op, LAST, side)]
    y_oppo = [move(14, oo, LAST, side, 0), move(15, oo, LAST, side, 1)]
    half_next = [move(16, nm, FIRST, up, 0), move(17, np_, FIRST, down, 1)]
    gathers = [y_first, y_last, *z_first, *z_last, *n_first, *half_first, *half_last, *y_near, *y_oppo, *half_next]
    for copy in (y_first, *z_last, *z_first, y_last):
        copy.start()
    ids = [
        pltpu.make_async_remote_copy(
            src_ref=E.at[h], dst_ref=E.at[h], send_sem=ess.at[j], recv_sem=ers.at[j],
            device_id=device, device_id_type=MESH,
        )
        for j, device in enumerate(group)
    ]
    for copy in ids:
        copy.start()
    half_rows = pl.ds(pl.multiple_of(c * 256, 256), 256)
    wo_far = send(18, wo_h.at[half_rows], WO.at[1, half_rows], far)
    wo_far.start()
    wo_twin = send(19, WO.at[1, half_rows], WO.at[1, half_rows], twin)

    pads = lax.broadcasted_iota(jnp.int32, (FEATS, HD), 0)
    def clear(slot, _):
        KV[slot] = jnp.zeros((KROWS + HD, HD), BF16)
        KV[slot, HD:KROWS, :] = jnp.where(pads == 8, 1.0, 0.0).astype(BF16)
        return 0

    lax.fori_loop(0, PAD, clear, 0)

    def chunk_of(i):
        stage, second = i // 2, i % 2
        col = jnp.where(stage == 0, jnp.where(second == 0, y, 1 - y),
              jnp.where(stage == 1, y,
              jnp.where(stage == 2, 1 - y, jnp.where(second == 0, y, 1 - y))))
        row = jnp.where(stage == 0, z, jnp.where(stage == 3, zo, jnp.where(second == 0, zm, zp)))
        return col * 4 + row

    def kv_copy(kind, i):
        g = chunk_of(i)
        quad = [x, x, x, (x + 3) % 4, (x + 2) % 4][kind]
        device = [twin, ring[1], ring[2], twin, twin][kind]
        slot = (quad * 2 + c) * 8 + g + PAD
        return pltpu.make_async_remote_copy(
            src_ref=KV.at[slot], dst_ref=KV.at[slot], send_sem=kss.at[kind, i],
            recv_sem=krs.at[kind, i], device_id=device, device_id_type=MESH,
        )

    lane = lax.broadcasted_iota(jnp.int32, (ROWS, HD), 1)
    scale = math.log2(math.e) / math.sqrt(HD)

    def project(items):
        pair = [chunk_of(i) for i in items]
        rows = jnp.concatenate([X[g, :, 0:D] for g in pair], axis=0)
        turns = []
        for g in pair:
            rc = b * 8 + g
            bc, bs = base_cos[pl.ds(rc, 1), :], base_sin[pl.ds(rc, 1), :]
            cosine = bc * step_cos[...] - bs * step_sin[...]
            sine = bs * step_cos[...] + bc * step_sin[...]
            turns.append((cosine, jnp.where(lane < 64, -sine, sine)))
        kv = dot(rows, WKV[...])
        for k, g in enumerate(pair):
            cosine, sine = turns[k]
            slot = b * 8 + g + PAD
            key = kv[k * ROWS : (k + 1) * ROWS, 0:HD]
            key = key * cosine + pltpu.roll(key, 64, 1) * sine
            KV[slot, 0:HD, :] = key.T.astype(BF16)
            KV[slot, HD:KROWS, :] = E[g]
            KV[slot, KROWS : KROWS + HD, :] = kv[k * ROWS : (k + 1) * ROWS, HD : 2 * HD].astype(BF16)
        for i in items:
            for kind in range(3):
                kv_copy(kind, i).start()
        for n in range(2):
            part = dot(rows, WQ[:, n * 256 : (n + 1) * 256])
            for k, g in enumerate(pair):
                cosine, sine = turns[k]
                for m in range(2):
                    head = part[k * ROWS : (k + 1) * ROWS, m * HD : (m + 1) * HD]
                    head = (head * cosine + pltpu.roll(head, 64, 1) * sine) * scale
                    for half in range(2):
                        at = half * 256 + (n * 2 + m) * 64
                        QE[g, at : at + 64, 0:HD] = head[half * 64 : half * 64 + 64].astype(BF16)
        for g in pair:
            mine = jnp.concatenate([E[g].astype(F32), jnp.zeros((ROWS - FEATS, ROWS), F32)], axis=0).T
            ext = jnp.where(lane < 8, jnp.where(mine > 0.5, 0.0, -BIG), jnp.where(lane == 8, -BIG, 0.0))
            for m in range(8):
                at = (m // 4) * 64
                QE[g, m * 64 : m * 64 + 64, HD : 2 * HD] = ext[at : at + 64].astype(BF16)

    def forward_kv(items):
        for i in items:
            for kind in (1, 2):
                kv_copy(kind, i).wait_recv()
                kv_copy(kind + 2, i).start()

    for load in loads[:3]:
        load.wait()

    pick_row = lax.broadcasted_iota(jnp.int32, (128, 512), 0)
    pick_col = lax.broadcasted_iota(jnp.int32, (128, 512), 1)
    chosen = (pick_col == (pick_row // 32) * 128 + z * 32 + pick_row % 32)
    chosen = jnp.where(chosen, 1.0, 0.0).astype(BF16)

    def tile_copy(kind, n, src, dst, device):
        return pltpu.make_async_remote_copy(
            src_ref=src, dst_ref=dst, send_sem=gss.at[kind, n], recv_sem=grs.at[kind, n],
            device_id=device, device_id_type=MESH,
        )

    def tile_at(n):
        return pl.ds(pl.multiple_of(n * TILE, TILE), TILE)

    def gram_twin(n):
        return tile_copy(0, n, GP.at[1 - c, :, tile_at(n)], GC.at[:, tile_at(n)], twin)

    def gram_ring(n):
        return [tile_copy(k, n, GP.at[c, pl.ds(pl.multiple_of(((x + k) % 4) * 64, 64), 64), tile_at(n)],
                          GX.at[k - 1, :, tile_at(n)], ring[k]) for k in (1, 2, 3)]

    def gram_other(n):
        rows = pl.ds(pl.multiple_of((1 - a) * 32, 32), 32)
        return tile_copy(4, n, GT.at[rows, tile_at(n)], GD.at[:, tile_at(n)], other)

    def gram_rows(last):
        slabs = [chunk_of(i) for i in ((6, 7) if last else range(6))]
        count = len(slabs) * ROWS
        for group in range(4):
            parts = []
            for n in range(4):
                q = (n % 2) * 8 + (2 * (group % 2) + n // 2) * 2 + group // 2
                at = pl.ds(pl.multiple_of(q * 256 + y * 128, 128), 128)
                parts.append(jnp.concatenate([X[g, :, at] for g in slabs], axis=0))
            taken = jnp.concatenate(parts, axis=1)
            picked = dot(chosen, taken, (((1,), (1,)), ((), ())))
            PKT[group * 128 : (group + 1) * 128, 0:count] = picked.astype(BF16)

        def gram_tile(n, _):
            at = pl.ds(pl.multiple_of(n * TILE, TILE), TILE)
            tile = dot(PKT[:, 0:count], jnp.concatenate([X[g, :, at] for g in slabs], axis=0))
            if last:
                GP[0, :, at] = (tile[0:256] + S0[:, at]).astype(BF16)
                GP[1, :, at] = (tile[256:512] + S1[:, at]).astype(BF16)
                gram_twin(n).start()
            else:
                S0[:, at] = tile[0:256]
                S1[:, at] = tile[256:512]
            return 0

        lax.fori_loop(0, D // TILE, gram_tile, 0)

    def gather_stage(stage, _):
        @pl.when(stage == 0)
        def _():
            for k in (0, 1):
                z_last[k].wait_recv()
                half_last[k].start()
                y_near[k].start()
            y_first.wait_recv()
            for k in (0, 1):
                n_first[k].start()
            for k in (0, 1):
                z_first[k].wait_recv()
                half_first[k].start()
            y_last.wait_recv()
            for copy in ids:
                copy.wait_recv()

        @pl.when(stage == 1)
        def _():
            for k in (0, 1):
                half_last[k].wait_recv()
                y_oppo[k].start()

        @pl.when(stage == 2)
        def _():
            for k in (0, 1):
                n_first[k].wait_recv()
                half_next[k].start()
            for copy in y_near:
                copy.wait_recv()

        project((2 * stage, 2 * stage + 1))

        @pl.when(stage > 0)
        def _():
            forward_kv((2 * stage - 2, 2 * stage - 1))

        return 0

    lax.fori_loop(0, 3, gather_stage, 0)
    gram_rows(False)
    forward_kv((4, 5))

    def gather_last(i, _):
        @pl.when(i == 0)
        def _():
            for copy in half_first:
                copy.wait_recv()

        @pl.when(i == 1)
        def _():
            for copy in (*half_next, *y_oppo):
                copy.wait_recv()

        project((6 + i,))
        return 0

    lax.fori_loop(0, 2, gather_last, 0)
    forward_kv((6,))

    wo_far.wait_recv()
    wo_twin.start()
    gram_rows(True)
    forward_kv((7,))

    def settle(i, _):
        kv_copy(0, i).wait_recv()
        kv_copy(3, i).wait_recv()
        kv_copy(4, i).wait_recv()
        return 0

    lax.fori_loop(0, 8, settle, 0)
    wo_twin.wait_recv()
    loads[3].wait()

    late = lax.broadcasted_iota(jnp.int32, (256, HD), 0) % 64 - lax.broadcasted_iota(jnp.int32, (256, HD), 1)
    blank = jnp.zeros((256 - KROWS, HD), BF16)
    ones = jnp.ones((HD, HD), BF16)
    steps = jnp.minimum(32 // SPAN, (8 * b + 7 + SPAN) // SPAN)

    def rows_of(half):
        return pl.ds(pl.multiple_of(half * 256, 256), 256)

    def keys_of(slot):
        return jnp.concatenate([KV[slot, 0:KROWS, :], blank], axis=0)

    def values_of(slot):
        return jnp.concatenate([KV[slot, KROWS : KROWS + HD, :], ones], axis=1)

    def score_first(g, half, S, MX):
        scores = jnp.where(late + half * 64 >= 0, dot(QE[g, rows_of(half), :], keys_of(b * 8 + g + PAD)), -BIG)
        S[:, WINDOW : WINDOW + HD] = scores
        MX[...] = scores

    def score_step(g, half, S, MX, t):
        first = b * 8 + g + PAD - SPAN * (t + 1)
        keys = jnp.concatenate([keys_of(first + j) for j in range(SPAN)], axis=1)
        scores = dot(QE[g, rows_of(half), :], keys)
        S[:, pl.ds(pl.multiple_of(t * SPAN * HD, SPAN * HD), SPAN * HD)] = scores
        top = MX[...]
        for j in range(SPAN):
            top = jnp.maximum(top, scores[:, j * HD : (j + 1) * HD])
        MX[...] = top

    def mix_first(g, S, MX):
        top = jnp.max(MX[...], axis=1, keepdims=True)
        TOP[...] = jnp.broadcast_to(top, (256, HD))
        probs = jnp.exp2(S[:, WINDOW : WINDOW + HD] - TOP[...]).astype(BF16)
        ACC[...] = dot(probs, values_of(b * 8 + g + PAD))

    def mix_step(g, S, t):
        first = b * 8 + g + PAD - SPAN * (t + 1)
        values = jnp.concatenate([values_of(first + j) for j in range(SPAN)], axis=0)
        scores = S[:, pl.ds(pl.multiple_of(t * SPAN * HD, SPAN * HD), SPAN * HD)]
        top = TOP[...]
        probs = jnp.concatenate(
            [jnp.exp2(scores[:, j * HD : (j + 1) * HD] - top).astype(BF16) for j in range(SPAN)], axis=1)
        ACC[...] += dot(probs, values)

    def mix_last(g, half):
        mixed = (ACC[:, 0:HD] / ACC[:, HD : 2 * HD]).astype(BF16)
        rows = pl.ds(pl.multiple_of(half * 64, 64), 64)
        for m in range(4):
            AT[g, rows, m * HD : (m + 1) * HD] = mixed[m * 64 : m * 64 + 64]

    def both(g, half, S, MX, next_g, next_half, next_S, next_MX):
        mix_first(g, S, MX)
        score_first(next_g, next_half, next_S, next_MX)

        def step(t, _):
            score_step(next_g, next_half, next_S, next_MX, t)
            mix_step(g, S, t)
            return 0

        lax.fori_loop(0, steps, step, 0)
        mix_last(g, half)

    top, low = pl.ds(0, 64), pl.ds(64, 64)

    def turned(kind, n):
        at = pl.ds(pl.multiple_of(n * OUT, OUT), OUT)
        src = PT.at[kind // 2, low if kind % 2 else top, at]
        dst = [
            RA.at[0, :, at], RA.at[1, :, at], RF.at[0, low, at],
            RF.at[1, top, at], RF.at[0, top, at], RF.at[1, low, at],
        ][kind]
        return pltpu.make_async_remote_copy(
            src_ref=src, dst_ref=dst, send_sem=tss.at[kind, n], recv_sem=trs.at[kind, n],
            device_id=down if kind % 2 else up, device_id_type=MESH,
        )

    def part_of(k, second):
        row = jnp.where(k == 0, zo, jnp.where(k == 3, z, jnp.where(second == 0, zp, zm)))
        half = jnp.where(k == 1, 1 - second, second)
        return row, half

    def swap(k, second):
        row, half = part_of(k, second)
        rows = pl.ds(pl.multiple_of(half * 64, 64), 64)
        to = pl.ds(pl.multiple_of(second * 64, 64), 64)
        return pltpu.make_async_remote_copy(
            src_ref=AT.at[(1 - y) * 4 + row, rows], dst_ref=AR.at[k, to], send_sem=sws.at[k, second],
            recv_sem=swr.at[k, second], device_id=side, device_id_type=MESH,
        )

    def gram_cores():
        def add(n, _):
            gram_twin(n).wait_recv()
            at = tile_at(n)
            GP[c, :, at] = (GP[c, :, at].astype(F32) + GC[:, at].astype(F32)).astype(BF16)
            for copy in gram_ring(n):
                copy.start()
            return 0

        lax.fori_loop(0, D // TILE, add, 0)

    def gram_quads(n):
        for copy in gram_ring(n):
            copy.wait_recv()
        at = tile_at(n)
        total = GP[c, pl.ds(pl.multiple_of(x * 64, 64), 64), at].astype(F32)
        for i in range(3):
            total = total + GX[i, :, at].astype(F32)
        GT[:, at] = total.astype(BF16)
        gram_other(n).start()

    def out_stage(k, _):
        rows = [part_of(k, 0), part_of(k, 1)]

        def unit(i, _):
            col = jnp.where(i == 0, 1 - y, y) * 4
            after = jnp.minimum(2 * k + i + 1, 7)
            after_col = jnp.where(after % 2 == 0, 1 - y, y) * 4
            after_row, after_half = part_of(after // 2, 0)
            both(col + rows[0][0], rows[0][1], S0, M0, col + rows[1][0], rows[1][1], S1, M1)

            @pl.when(i == 0)
            def _():
                swap(k, 0).start()

            both(col + rows[1][0], rows[1][1], S1, M1, after_col + after_row, after_half, S0, M0)

            @pl.when(i == 0)
            def _():
                swap(k, 1).start()

            @pl.when((i == 0) & (k == 0))
            def _():
                gram_cores()

            @pl.when((k == 1) | (k == 2))
            def _():
                gram_quads(2 * k - 2 + i)

            return 0

        lax.fori_loop(0, 2, unit, 0)
        swap(k, 0).wait_recv()
        swap(k, 1).wait_recv()
        own = jnp.concatenate(
            [AT[y * 4 + row, pl.ds(pl.multiple_of(half * 64, 64), 64), :] for row, half in rows], axis=0)

        def out_tile(n, _):
            at = pl.ds(pl.multiple_of(n * OUT, OUT), OUT)
            part = dot(own, WO[0, :, at]) + dot(AR[k], WO[1, :, at])

            @pl.when(k != 2)
            def _():
                PT[k, :, at] = part.astype(BF16)

            @pl.when(k == 2)
            def _():
                for which, rows in enumerate((top, low)):
                    turned(which, n).wait_recv()
                    first = 64 * which
                    PT[2, rows, at] = (part[first : first + 64] + RA[which, :, at].astype(F32)).astype(BF16)

            for stage in range(3):
                @pl.when(k == stage)
                def _(stage=stage):
                    turned(2 * stage, n).start()
                    turned(2 * stage + 1, n).start()

            return 0

        lax.fori_loop(0, D // OUT, out_tile, 0)
        return 0

    start_g = (1 - y) * 4 + zo
    score_first(start_g, 0, S0, M0)

    def start_step(t, _):
        score_step(start_g, 0, S0, M0, t)
        return 0

    lax.fori_loop(0, steps, start_step, 0)
    lax.fori_loop(0, 4, out_stage, 0)
    mine = pl.ds(pl.multiple_of(a * 32, 32), 32)
    for n in range(D // TILE):
        gram_other(n).wait_recv()
    gram[...] = GT[mine, :].astype(F32) + GD[...].astype(F32)

    def total(n, _):
        at = pl.ds(pl.multiple_of(n * OUT, OUT), OUT)
        for kind in range(2, 6):
            turned(kind, n).wait_recv()
        out[:, at] = (PT[3, :, at].astype(F32) + RF[0, :, at].astype(F32) + RF[1, :, at].astype(F32)).astype(BF16)
        return 0

    lax.fori_loop(0, D // OUT, total, 0)

    for copy in [*gathers, *ids, wo_far, wo_twin]:
        copy.wait_send()

    def drain(i, _):
        for kind in range(5):
            kv_copy(kind, i).wait_send()
        return 0

    lax.fori_loop(0, 8, drain, 0)

    def drain_gram(n, _):
        for copy in (gram_twin(n), *gram_ring(n), gram_other(n)):
            copy.wait_send()
        return 0

    def drain_turned(n, _):
        for kind in range(6):
            turned(kind, n).wait_send()
        return 0

    lax.fori_loop(0, D // OUT, drain_turned, 0)

    lax.fori_loop(0, D // TILE, drain_gram, 0)

    def drain_swap(k, _):
        swap(k, 0).wait_send()
        swap(k, 1).wait_send()
        return 0

    lax.fori_loop(0, 4, drain_swap, 0)


def finish(delta, gram, delta_out, gram_out):
    delta_out[...] = delta[...]
    gram_out[...] = gram[...] * (1.0 / 16384.0)


def per_device(tokens, norm_gain, segment_ids, w_query, w_key, w_value, w_out):
    vmem = pl.BlockSpec(memory_space=pltpu.VMEM)
    hbm = pl.BlockSpec(memory_space=pl.ANY)
    dma = pltpu.SemaphoreType.DMA
    scratch = [
        pltpu.VMEM((8, ROWS, D), BF16),
        pltpu.VMEM((8, FEATS, ROWS), BF16),
        pltpu.VMEM((ROWS, D), BF16),
        pltpu.VMEM((D, 512), BF16),
        pltpu.VMEM((D, 256), BF16),
        pltpu.VMEM((2, 512, D), BF16),
        pltpu.VMEM((8, 512, 256), BF16),
        pltpu.VMEM((64 + PAD, KROWS + HD, HD), BF16),
        pltpu.VMEM((512, 768), BF16),
        pltpu.VMEM((2, 256, D), BF16),
        pltpu.VMEM((256, D), BF16),
        pltpu.VMEM((3, 64, D), BF16),
        pltpu.VMEM((64, D), BF16),
        pltpu.VMEM((32, D), BF16),
        pltpu.VMEM((8, ROWS, 512), BF16),
        pltpu.VMEM((4, ROWS, 512), BF16),
        pltpu.VMEM((4, ROWS, D), BF16),
        pltpu.VMEM((2, 64, D), BF16),
        pltpu.VMEM((2, ROWS, D), BF16),
        pltpu.VMEM((256, 256), F32),
        pltpu.VMEM((256, HD), F32),
        pltpu.VMEM((256, WINDOW + HD), F32),
        pltpu.VMEM((256, WINDOW + HD), F32),
        pltpu.VMEM((256, HD), F32),
        pltpu.VMEM((256, HD), F32),
        dma((40,)),
        dma((40,)),
        dma((5, 8)),
        dma((5, 8)),
        dma((4, 2)),
        dma((4, 2)),
        dma((5, 4)),
        dma((5, 4)),
        dma((7,)),
        dma((7,)),
        dma((6, 2)),
        dma((6, 2)),
        dma((5,)),
    ]
    delta, gram = pl.pallas_call(
        kernel,
        out_shape=(jax.ShapeDtypeStruct((ROWS, D), BF16), jax.ShapeDtypeStruct((32, D), F32)),
        in_specs=[hbm, vmem, vmem, hbm, hbm, hbm, hbm, vmem, vmem, vmem, vmem],
        out_specs=(vmem, vmem),
        scratch_shapes=scratch,
        compiler_params=pltpu.CompilerParams(
            collective_id=0, has_side_effects=True, vmem_limit_bytes=62 << 20),
        name="sublayer",
    )(tokens[0], norm_gain[None], segment_ids, w_query, w_key, w_value, w_out,
      *[jnp.asarray(t) for t in tables()])
    delta, gram = pl.pallas_call(
        finish,
        out_shape=(jax.ShapeDtypeStruct((ROWS, D), BF16), jax.ShapeDtypeStruct((32, D), F32)),
        in_specs=[vmem, vmem],
        out_specs=(vmem, vmem),
        name="finish",
    )(delta, gram)
    return delta[None], gram


def solution(mesh):
    return jax.shard_map(
        per_device,
        mesh=mesh,
        in_specs=(
            P("dp", ("blk", "heads"), None),
            P(),
            P("dp", ("blk", "heads")),
            P(None, "heads"),
            P(None, "heads"),
            P(None, "heads"),
            P("heads", None),
        ),
        out_specs=(P("dp", ("blk", "heads"), None), P(("dp", "blk", "heads"), None)),
        check_vma=False,
    )
```

```python
import math

import jax
import jax.numpy as jnp
import numpy as np
from jax import lax
from jax.experimental import pallas as pl
from jax.experimental.pallas import tpu as pltpu
from jax.sharding import PartitionSpec as P

MESH = pl.DeviceIdType.MESH
HD = 128
D = 4096
ROWS = 128
EPSILON = 1e-05
ROPE_BASE = 500000.0
BIG = 1e30
FEATS = 16
KROWS = HD + FEATS
SPAN = 16
OUT = 2048
TILE = 1024
PAD = SPAN
CUT = 18 * 128
WINDOW = 4096
F32 = jnp.float32
BF16 = jnp.bfloat16


def tables():
    frequency = ROPE_BASE ** (-(np.arange(64, dtype=np.float64) * 2.0 / HD))
    frequency = np.concatenate([frequency, frequency])
    base = np.arange(64)[:, None] * float(ROWS) * frequency[None, :]
    step = np.arange(ROWS)[:, None] * frequency[None, :]
    return [f(v).astype(np.float32) for v in (base, step) for f in (np.cos, np.sin)]


def dot(a, b, dims=(((1,), (0,)), ((), ()))):
    return lax.dot_general(a, b, dims, preferred_element_type=F32)


def kernel(
    tok_h, gain, seg, wq_h, wk_h, wv_h, wo_h, base_cos, base_sin, step_cos, step_sin,
    out, gram,
    X, E, tok, WQ, WKV, WO, QE, KV, PKT, GP, GC, GX, GT, GD, AT, AR, PT, RA, RF, ACC, TOP, S0, S1, M0, M1,
    ss, rs, kss, krs, sws, swr, gss, grs, ess, ers, tss, trs, ras, rar, ls,
):
    a, b, h = lax.axis_index("dp"), lax.axis_index("blk"), lax.axis_index("heads")
    x, c = b // 2, b % 2
    y, z = h // 4, h % 4
    zp, zm, zo = (z + 1) % 4, (z + 3) % 4, (z + 2) % 4
    up, down = (a, b, y * 4 + zp), (a, b, y * 4 + zm)
    side = (a, b, (1 - y) * 4 + z)
    far = (1 - a, b, (1 - y) * 4 + z)
    twin = (a, x * 2 + 1 - c, h)
    other = (1 - a, b, h)
    ring = [None] + [(a, ((x + k) % 4) * 2 + c, h) for k in (1, 2, 3)]

    load_tok = pltpu.make_async_copy(tok_h, tok, ls.at[4])
    load_tok.start()
    loads = [
        pltpu.make_async_copy(wk_h, WKV.at[:, 0:HD], ls.at[0]),
        pltpu.make_async_copy(wv_h, WKV.at[:, HD : 2 * HD], ls.at[1]),
        pltpu.make_async_copy(wq_h, WQ, ls.at[2]),
        pltpu.make_async_copy(wo_h, WO.at[0], ls.at[3]),
    ]
    barrier = pltpu.get_barrier_semaphore()
    group = [(a, b, ((y + j // 4) % 2) * 4 + (z + j) % 4) for j in range(1, 8)]
    partners = group + [far, twin, other] + ring[1:]
    for partner in partners:
        pl.semaphore_signal(barrier, inc=1, device_id=partner, device_id_type=MESH)

    load_tok.wait()
    for load in loads:
        load.start()

    def normalise(i, _):
        at = pl.ds(pl.multiple_of(i * 16, 16), 16)
        values = tok[at, :].astype(F32)
        mean_square = jnp.mean(values * values, axis=-1, keepdims=True)
        X[h, at, 0:D] = (values * lax.rsqrt(mean_square + EPSILON) * gain[...]).astype(BF16)
        return 0

    lax.fori_loop(0, ROWS // 16, normalise, 0)
    feature = lax.broadcasted_iota(jnp.int32, (FEATS, ROWS), 0)
    E[h] = jnp.where(feature == seg[...], 1.0, 0.0).astype(BF16)

    pl.semaphore_wait(barrier, len(partners))

    def send(i, src, dst, device):
        return pltpu.make_async_remote_copy(
            src_ref=src, dst_ref=dst, send_sem=ss.at[i], recv_sem=rs.at[i],
            device_id=device, device_id_type=MESH,
        )

    FIRST, LAST = pl.ds(0, CUT), pl.ds(CUT, D - CUT)

    def move(i, g, columns, device, half=None):
        rows = pl.ds(0, ROWS) if half is None else pl.ds(half * 64, 64)
        return send(i, X.at[g, rows, columns], X.at[g, rows, columns], device)

    hs = (1 - y) * 4 + z
    om, op, oo = y * 4 + zm, y * 4 + zp, y * 4 + zo
    nm, np_ = (1 - y) * 4 + zm, (1 - y) * 4 + zp
    y_first = move(0, h, FIRST, side)
    y_last = move(1, h, LAST, side)
    z_first = [move(2, h, FIRST, up), move(3, h, FIRST, down)]
    z_last = [move(4, h, LAST, up), move(5, h, LAST, down)]
    n_first = [move(6, hs, FIRST, up), move(7, hs, FIRST, down)]
    half_first = [move(8, om, FIRST, up, 0), move(9, op, FIRST, down, 1)]
    half_last = [move(10, om, LAST, up, 0), move(11, op, LAST, down, 1)]
    y_near = [move(12, om, LAST, side), move(13, op, LAST, side)]
    y_oppo = [move(14, oo, LAST, side, 0), move(15, oo, LAST, side, 1)]
    half_next = [move(16, nm, FIRST, up, 0), move(17, np_, FIRST, down, 1)]
    gathers = [y_first, y_last, *z_first, *z_last, *n_first, *half_first, *half_last, *y_near, *y_oppo, *half_next]
    for copy in (y_first, *z_last, *z_first, y_last):
        copy.start()
    ids = [
        pltpu.make_async_remote_copy(
            src_ref=E.at[h], dst_ref=E.at[h], send_sem=ess.at[j], recv_sem=ers.at[j],
            device_id=device, device_id_type=MESH,
        )
        for j, device in enumerate(group)
    ]
    for copy in ids:
        copy.start()
    half_rows = pl.ds(pl.multiple_of(c * 256, 256), 256)
    wo_far = send(18, wo_h.at[half_rows], WO.at[1, half_rows], far)
    wo_far.start()
    wo_twin = send(19, WO.at[1, half_rows], WO.at[1, half_rows], twin)

    pads = lax.broadcasted_iota(jnp.int32, (FEATS, HD), 0)
    def clear(slot, _):
        KV[slot] = jnp.zeros((KROWS + HD, HD), BF16)
        KV[slot, HD:KROWS, :] = jnp.where(pads == 8, 1.0, 0.0).astype(BF16)
        return 0

    lax.fori_loop(0, PAD, clear, 0)

    def chunk_of(i):
        stage, second = i // 2, i % 2
        col = jnp.where(stage == 0, jnp.where(second == 0, y, 1 - y),
              jnp.where(stage == 1, y,
              jnp.where(stage == 2, 1 - y, jnp.where(second == 0, y, 1 - y))))
        row = jnp.where(stage == 0, z, jnp.where(stage == 3, zo, jnp.where(second == 0, zm, zp)))
        return col * 4 + row

    def kv_copy(kind, i):
        g = chunk_of(i)
        quad = [x, x, x, (x + 3) % 4, (x + 2) % 4][kind]
        device = [twin, ring[1], ring[2], twin, twin][kind]
        slot = (quad * 2 + c) * 8 + g + PAD
        return pltpu.make_async_remote_copy(
            src_ref=KV.at[slot], dst_ref=KV.at[slot], send_sem=kss.at[kind, i],
            recv_sem=krs.at[kind, i], device_id=device, device_id_type=MESH,
        )

    lane = lax.broadcasted_iota(jnp.int32, (ROWS, HD), 1)
    scale = math.log2(math.e) / math.sqrt(HD)

    def project(items):
        pair = [chunk_of(i) for i in items]
        rows = jnp.concatenate([X[g, :, 0:D] for g in pair], axis=0)
        turns = []
        for g in pair:
            rc = b * 8 + g
            bc, bs = base_cos[pl.ds(rc, 1), :], base_sin[pl.ds(rc, 1), :]
            cosine = bc * step_cos[...] - bs * step_sin[...]
            sine = bs * step_cos[...] + bc * step_sin[...]
            turns.append((cosine, jnp.where(lane < 64, -sine, sine)))
        kv = dot(rows, WKV[...])
        for k, g in enumerate(pair):
            cosine, sine = turns[k]
            slot = b * 8 + g + PAD
            key = kv[k * ROWS : (k + 1) * ROWS, 0:HD]
            key = key * cosine + pltpu.roll(key, 64, 1) * sine
            KV[slot, 0:HD, :] = key.T.astype(BF16)
            KV[slot, HD:KROWS, :] = E[g]
            KV[slot, KROWS : KROWS + HD, :] = kv[k * ROWS : (k + 1) * ROWS, HD : 2 * HD].astype(BF16)
        for i in items:
            for kind in range(3):
                kv_copy(kind, i).start()
        for n in range(2):
            part = dot(rows, WQ[:, n * 256 : (n + 1) * 256])
            for k, g in enumerate(pair):
                cosine, sine = turns[k]
                for m in range(2):
                    head = part[k * ROWS : (k + 1) * ROWS, m * HD : (m + 1) * HD]
                    head = (head * cosine + pltpu.roll(head, 64, 1) * sine) * scale
                    for part_at in range(4):
                        at = part_at * 128 + (n * 2 + m) * 32
                        QE[g, at : at + 32, 0:HD] = head[part_at * 32 : part_at * 32 + 32].astype(BF16)
        for g in pair:
            mine = jnp.concatenate([E[g].astype(F32), jnp.zeros((ROWS - FEATS, ROWS), F32)], axis=0).T
            ext = jnp.where(lane < 8, jnp.where(mine > 0.5, 0.0, -BIG), jnp.where(lane == 8, -BIG, 0.0))
            for m in range(16):
                at = (m // 4) * 32
                QE[g, m * 32 : m * 32 + 32, HD : 2 * HD] = ext[at : at + 32].astype(BF16)

    def forward_kv(items):
        for i in items:
            for kind in (1, 2):
                kv_copy(kind, i).wait_recv()
                kv_copy(kind + 2, i).start()

    for load in loads[:3]:
        load.wait()

    pick_row = lax.broadcasted_iota(jnp.int32, (128, 512), 0)
    pick_col = lax.broadcasted_iota(jnp.int32, (128, 512), 1)
    chosen = (pick_col == (pick_row // 32) * 128 + z * 32 + pick_row % 32)
    chosen = jnp.where(chosen, 1.0, 0.0).astype(BF16)

    def tile_copy(kind, n, src, dst, device):
        return pltpu.make_async_remote_copy(
            src_ref=src, dst_ref=dst, send_sem=gss.at[kind, n], recv_sem=grs.at[kind, n],
            device_id=device, device_id_type=MESH,
        )

    def tile_at(n):
        return pl.ds(pl.multiple_of(n * TILE, TILE), TILE)

    def gram_twin(n):
        return tile_copy(0, n, GP.at[1 - c, :, tile_at(n)], GC.at[:, tile_at(n)], twin)

    def gram_ring(n):
        return [tile_copy(k, n, GP.at[c, pl.ds(pl.multiple_of(((x + k) % 4) * 64, 64), 64), tile_at(n)],
                          GX.at[k - 1, :, tile_at(n)], ring[k]) for k in (1, 2, 3)]

    def gram_other(n):
        rows = pl.ds(pl.multiple_of((1 - a) * 32, 32), 32)
        return tile_copy(4, n, GT.at[rows, tile_at(n)], GD.at[:, tile_at(n)], other)

    def gram_rows(last):
        slabs = [chunk_of(i) for i in ((6, 7) if last else range(6))]
        count = len(slabs) * ROWS
        for group in range(4):
            parts = []
            for n in range(4):
                q = (n % 2) * 8 + (2 * (group % 2) + n // 2) * 2 + group // 2
                at = pl.ds(pl.multiple_of(q * 256 + y * 128, 128), 128)
                parts.append(jnp.concatenate([X[g, :, at] for g in slabs], axis=0))
            taken = jnp.concatenate(parts, axis=1)
            picked = dot(chosen, taken, (((1,), (1,)), ((), ())))
            PKT[group * 128 : (group + 1) * 128, 0:count] = picked.astype(BF16)

        def gram_tile(n, _):
            at = pl.ds(pl.multiple_of(n * TILE, TILE), TILE)
            tile = dot(PKT[:, 0:count], jnp.concatenate([X[g, :, at] for g in slabs], axis=0))
            if last:
                GP[0, :, at] = (tile[0:256] + S0[:, at]).astype(BF16)
                GP[1, :, at] = (tile[256:512] + S1[:, at]).astype(BF16)
                gram_twin(n).start()
            else:
                S0[:, at] = tile[0:256]
                S1[:, at] = tile[256:512]
            return 0

        lax.fori_loop(0, D // TILE, gram_tile, 0)

    def gather_stage(stage, _):
        @pl.when(stage == 0)
        def _():
            for k in (0, 1):
                z_last[k].wait_recv()
                half_last[k].start()
                y_near[k].start()
            y_first.wait_recv()
            for k in (0, 1):
                n_first[k].start()
            for k in (0, 1):
                z_first[k].wait_recv()
                half_first[k].start()
            y_last.wait_recv()
            for copy in ids:
                copy.wait_recv()

        @pl.when(stage == 1)
        def _():
            for k in (0, 1):
                half_last[k].wait_recv()
                y_oppo[k].start()

        @pl.when(stage == 2)
        def _():
            for k in (0, 1):
                n_first[k].wait_recv()
                half_next[k].start()
            for copy in y_near:
                copy.wait_recv()

        project((2 * stage, 2 * stage + 1))

        @pl.when(stage > 0)
        def _():
            forward_kv((2 * stage - 2, 2 * stage - 1))

        return 0

    lax.fori_loop(0, 3, gather_stage, 0)
    gram_rows(False)
    forward_kv((4, 5))

    def gather_last(i, _):
        @pl.when(i == 0)
        def _():
            for copy in half_first:
                copy.wait_recv()

        @pl.when(i == 1)
        def _():
            for copy in (*half_next, *y_oppo):
                copy.wait_recv()

        project((6 + i,))
        return 0

    lax.fori_loop(0, 2, gather_last, 0)
    forward_kv((6,))

    wo_far.wait_recv()
    wo_twin.start()
    gram_rows(True)
    forward_kv((7,))

    def gram_cores():
        def add(n, _):
            gram_twin(n).wait_recv()
            at = tile_at(n)
            GP[c, :, at] = (GP[c, :, at].astype(F32) + GC[:, at].astype(F32)).astype(BF16)
            for copy in gram_ring(n):
                copy.start()
            return 0

        lax.fori_loop(0, D // TILE, add, 0)

    gram_cores()

    def settle(i, _):
        kv_copy(0, i).wait_recv()
        kv_copy(3, i).wait_recv()
        kv_copy(4, i).wait_recv()
        return 0

    lax.fori_loop(0, 8, settle, 0)
    wo_twin.wait_recv()
    loads[3].wait()

    row_in = lax.broadcasted_iota(jnp.int32, (256, HD), 0)
    late = row_in % 32 - lax.broadcasted_iota(jnp.int32, (256, HD), 1)
    second_quarter = row_in >= 128
    blank = jnp.zeros((256 - KROWS, HD), BF16)
    ones = jnp.ones((HD, HD), BF16)
    steps = jnp.minimum(32 // SPAN, (8 * b + 7 + SPAN) // SPAN)

    def queries_of(g, quarters):
        return jnp.concatenate(
            [QE[g, pl.ds(pl.multiple_of(q * 128, 128), 128), :] for q in quarters], axis=0)

    def keys_of(slot):
        return jnp.concatenate([KV[slot, 0:KROWS, :], blank], axis=0)

    def values_of(slot):
        return jnp.concatenate([KV[slot, KROWS : KROWS + HD, :], ones], axis=1)

    def score_first(g, half, S, MX):
        scores = jnp.where(late + jnp.where(second_quarter, half[1], half[0]) * 32 >= 0,
                           dot(queries_of(g, half), keys_of(b * 8 + g + PAD)), -BIG)
        S[:, WINDOW : WINDOW + HD] = scores
        MX[...] = scores

    def score_step(g, half, S, MX, t):
        first = b * 8 + g + PAD - SPAN * (t + 1)
        keys = jnp.concatenate([keys_of(first + j) for j in range(SPAN)], axis=1)
        scores = dot(queries_of(g, half), keys)
        S[:, pl.ds(pl.multiple_of(t * SPAN * HD, SPAN * HD), SPAN * HD)] = scores
        top = MX[...]
        for j in range(SPAN):
            top = jnp.maximum(top, scores[:, j * HD : (j + 1) * HD])
        MX[...] = top

    def mix_first(g, S, MX):
        top = jnp.max(MX[...], axis=1, keepdims=True)
        TOP[...] = jnp.broadcast_to(top, (256, HD))
        probs = jnp.exp2(S[:, WINDOW : WINDOW + HD] - TOP[...]).astype(BF16)
        ACC[...] = dot(probs, values_of(b * 8 + g + PAD))

    def mix_step(g, S, t):
        first = b * 8 + g + PAD - SPAN * (t + 1)
        values = jnp.concatenate([values_of(first + j) for j in range(SPAN)], axis=0)
        scores = S[:, pl.ds(pl.multiple_of(t * SPAN * HD, SPAN * HD), SPAN * HD)]
        top = TOP[...]
        probs = jnp.concatenate(
            [jnp.exp2(scores[:, j * HD : (j + 1) * HD] - top).astype(BF16) for j in range(SPAN)], axis=1)
        ACC[...] += dot(probs, values)

    def mix_last(place):
        mixed = (ACC[:, 0:HD] / ACC[:, HD : 2 * HD]).astype(BF16)
        own, k, second = place
        for m in range(8):
            rows = pl.ds(pl.multiple_of(second * 64 + (m // 4) * 32, 32), 32)
            AT[own * 4 + k, rows, (m % 4) * HD : (m % 4 + 1) * HD] = mixed[m * 32 : m * 32 + 32]

    def both(g, place, S, MX, next_g, next_half, next_S, next_MX):
        mix_first(g, S, MX)
        score_first(next_g, next_half, next_S, next_MX)

        def step(t, _):
            score_step(next_g, next_half, next_S, next_MX, t)
            mix_step(g, S, t)
            return 0

        lax.fori_loop(0, steps, step, 0)
        mix_last(place)

    top, low = pl.ds(0, 64), pl.ds(64, 64)

    def turned(kind, n):
        at = pl.ds(pl.multiple_of(n * OUT, OUT), OUT)
        src = PT.at[1 + kind // 2, low if kind % 2 else top, at]
        dst = [RF.at[0, low, at], RF.at[1, top, at], RF.at[0, top, at], RF.at[1, low, at]][kind]
        return pltpu.make_async_remote_copy(
            src_ref=src, dst_ref=dst, send_sem=tss.at[kind, n], recv_sem=trs.at[kind, n],
            device_id=down if kind % 2 else up, device_id_type=MESH,
        )

    def relayed(which, second, n):
        at = pl.ds(pl.multiple_of(n * OUT, OUT), OUT)
        rows = pl.ds(pl.multiple_of(second * 64 + which * 32, 32), 32)
        to = pl.ds(pl.multiple_of(second * 32, 32), 32)
        return pltpu.make_async_remote_copy(
            src_ref=PT.at[0, rows, at], dst_ref=RA.at[which, to, at], send_sem=ras.at[which, second, n],
            recv_sem=rar.at[which, second, n], device_id=down if which else up, device_id_type=MESH,
        )

    def part_of(k, second):
        row = jnp.where(k == 0, zo, jnp.where(k == 3, z, jnp.where(second == 0, zp, zm)))
        odd = jnp.where(k == 1, 1 - second, second)
        mixed = (k == 1) | (k == 2)
        first = jnp.where(mixed, odd, 2 * second)
        return row, (first, first + jnp.where(mixed, 2, 1))

    def swap(k, second):
        rows = pl.ds(pl.multiple_of(second * 64, 64), 64)
        return pltpu.make_async_remote_copy(
            src_ref=AT.at[k, rows], dst_ref=AR.at[k, rows], send_sem=sws.at[k, second],
            recv_sem=swr.at[k, second], device_id=side, device_id_type=MESH,
        )

    def gram_quads(n):
        for copy in gram_ring(n):
            copy.wait_recv()
        at = tile_at(n)
        total = GP[c, pl.ds(pl.multiple_of(x * 64, 64), 64), at].astype(F32)
        for i in range(3):
            total = total + GX[i, :, at].astype(F32)
        GT[:, at] = total.astype(BF16)
        gram_other(n).start()

    def item_of(i):
        k, j = i // 4, i % 4
        own = jnp.where(k == 0, j % 2, j // 2)
        second = jnp.where(k == 0, j // 2, j % 2)
        row, quarters = part_of(k, second)
        return jnp.where(own == 1, y, 1 - y) * 4 + row, quarters, (own, k, second)

    def project_out(k, rows, n):
        at = pl.ds(pl.multiple_of(n * OUT, OUT), OUT)
        return at, dot(AT[4 + k, rows, :], WO[0, :, at]) + dot(AR[k, rows, :], WO[1, :, at])

    def out_first(second):
        swap(0, second).wait_recv()

        def tile(n, _):
            rows = pl.ds(pl.multiple_of(second * 64, 64), 64)
            at, part = project_out(0, rows, n)
            PT[0, rows, at] = part.astype(BF16)
            relayed(0, second, n).start()
            relayed(1, second, n).start()
            return 0

        lax.fori_loop(0, D // OUT, tile, 0)

    def out_round(k):
        swap(k, 0).wait_recv()
        swap(k, 1).wait_recv()

        def tile(n, _):
            at, part = project_out(k, pl.ds(0, ROWS), n)

            @pl.when(k != 2)
            def _():
                PT[k, :, at] = part.astype(BF16)

            @pl.when(k == 2)
            def _():
                for which, rows in enumerate((top, low)):
                    relayed(which, 0, n).wait_recv()
                    relayed(which, 1, n).wait_recv()
                    first = 64 * which
                    PT[2, rows, at] = (part[first : first + 64] + RA[which, :, at].astype(F32)).astype(BF16)

            for stage in (1, 2):
                @pl.when(k == stage)
                def _(stage=stage):
                    turned(2 * stage - 2, n).start()
                    turned(2 * stage - 1, n).start()

            return 0

        lax.fori_loop(0, D // OUT, tile, 0)

    def item_pair(p, _):
        g0, quarters0, place0 = item_of(2 * p)
        g1, quarters1, place1 = item_of(2 * p + 1)
        g2, quarters2, _place = item_of(jnp.minimum(2 * p + 2, 15))
        both(g0, place0, S0, M0, g1, quarters1, S1, M1)

        @pl.when((p < 2) | (p % 2 == 0))
        def _():
            swap(place0[1], place0[2]).start()

        @pl.when(p == 1)
        def _():
            out_first(0)

        both(g1, place1, S1, M1, g2, quarters2, S0, M0)

        @pl.when((p >= 2) & (p % 2 == 0))
        def _():
            swap(place1[1], place1[2]).start()

        @pl.when(p == 1)
        def _():
            out_first(1)

        @pl.when((p >= 2) & (p < 6))
        def _():
            gram_quads(p - 2)

        @pl.when((p >= 2) & (p % 2 == 1))
        def _():
            out_round(p // 2)

        return 0

    start_g = (1 - y) * 4 + zo
    score_first(start_g, (0, 1), S0, M0)

    def start_step(t, _):
        score_step(start_g, (0, 1), S0, M0, t)
        return 0

    lax.fori_loop(0, steps, start_step, 0)
    lax.fori_loop(0, 8, item_pair, 0)
    mine = pl.ds(pl.multiple_of(a * 32, 32), 32)
    for n in range(D // TILE):
        gram_other(n).wait_recv()
    gram[...] = GT[mine, :].astype(F32) + GD[...].astype(F32)

    def total(n, _):
        at = pl.ds(pl.multiple_of(n * OUT, OUT), OUT)
        for kind in range(4):
            turned(kind, n).wait_recv()
        for q in range(4):
            to, given = pl.ds(q * 32, 32), pl.ds((q % 2) * 64 + (q // 2) * 32, 32)
            out[to, at] = (PT[3, to, at].astype(F32) + RF[0, given, at].astype(F32)
                           + RF[1, given, at].astype(F32)).astype(BF16)
        return 0

    lax.fori_loop(0, D // OUT, total, 0)

    for copy in [*gathers, *ids, wo_far, wo_twin]:
        copy.wait_send()

    def drain(i, _):
        for kind in range(5):
            kv_copy(kind, i).wait_send()
        return 0

    lax.fori_loop(0, 8, drain, 0)

    def drain_gram(n, _):
        for copy in (gram_twin(n), *gram_ring(n), gram_other(n)):
            copy.wait_send()
        return 0

    def drain_turned(n, _):
        for kind in range(4):
            turned(kind, n).wait_send()
        for which in range(2):
            for second in range(2):
                relayed(which, second, n).wait_send()
        return 0

    lax.fori_loop(0, D // OUT, drain_turned, 0)

    lax.fori_loop(0, D // TILE, drain_gram, 0)

    def drain_swap(k, _):
        swap(k, 0).wait_send()
        swap(k, 1).wait_send()
        return 0

    lax.fori_loop(0, 4, drain_swap, 0)


def finish(delta, gram, delta_out, gram_out):
    delta_out[...] = delta[...]
    gram_out[...] = gram[...] * (1.0 / 16384.0)


def per_device(tokens, norm_gain, segment_ids, w_query, w_key, w_value, w_out):
    vmem = pl.BlockSpec(memory_space=pltpu.VMEM)
    hbm = pl.BlockSpec(memory_space=pl.ANY)
    dma = pltpu.SemaphoreType.DMA
    scratch = [
        pltpu.VMEM((8, ROWS, D), BF16),
        pltpu.VMEM((8, FEATS, ROWS), BF16),
        pltpu.VMEM((ROWS, D), BF16),
        pltpu.VMEM((D, 512), BF16),
        pltpu.VMEM((D, 256), BF16),
        pltpu.VMEM((2, 512, D), BF16),
        pltpu.VMEM((8, 512, 256), BF16),
        pltpu.VMEM((64 + PAD, KROWS + HD, HD), BF16),
        pltpu.VMEM((512, 768), BF16),
        pltpu.VMEM((2, 256, D), BF16),
        pltpu.VMEM((256, D), BF16),
        pltpu.VMEM((3, 64, D), BF16),
        pltpu.VMEM((64, D), BF16),
        pltpu.VMEM((32, D), BF16),
        pltpu.VMEM((8, ROWS, 512), BF16),
        pltpu.VMEM((4, ROWS, 512), BF16),
        pltpu.VMEM((4, ROWS, D), BF16),
        pltpu.VMEM((2, 64, D), BF16),
        pltpu.VMEM((2, ROWS, D), BF16),
        pltpu.VMEM((256, 256), F32),
        pltpu.VMEM((256, HD), F32),
        pltpu.VMEM((256, WINDOW + HD), F32),
        pltpu.VMEM((256, WINDOW + HD), F32),
        pltpu.VMEM((256, HD), F32),
        pltpu.VMEM((256, HD), F32),
        dma((40,)),
        dma((40,)),
        dma((5, 8)),
        dma((5, 8)),
        dma((4, 2)),
        dma((4, 2)),
        dma((5, 4)),
        dma((5, 4)),
        dma((7,)),
        dma((7,)),
        dma((4, 2)),
        dma((4, 2)),
        dma((2, 2, 2)),
        dma((2, 2, 2)),
        dma((5,)),
    ]
    delta, gram = pl.pallas_call(
        kernel,
        out_shape=(jax.ShapeDtypeStruct((ROWS, D), BF16), jax.ShapeDtypeStruct((32, D), F32)),
        in_specs=[hbm, vmem, vmem, hbm, hbm, hbm, hbm, vmem, vmem, vmem, vmem],
        out_specs=(vmem, vmem),
        scratch_shapes=scratch,
        compiler_params=pltpu.CompilerParams(
            collective_id=0, has_side_effects=True, vmem_limit_bytes=62 << 20),
        name="sublayer",
    )(tokens[0], norm_gain[None], segment_ids, w_query, w_key, w_value, w_out,
      *[jnp.asarray(t) for t in tables()])
    delta, gram = pl.pallas_call(
        finish,
        out_shape=(jax.ShapeDtypeStruct((ROWS, D), BF16), jax.ShapeDtypeStruct((32, D), F32)),
        in_specs=[vmem, vmem],
        out_specs=(vmem, vmem),
        name="finish",
    )(delta, gram)
    return delta[None], gram


def solution(mesh):
    return jax.shard_map(
        per_device,
        mesh=mesh,
        in_specs=(
            P("dp", ("blk", "heads"), None),
            P(),
            P("dp", ("blk", "heads")),
            P(None, "heads"),
            P(None, "heads"),
            P(None, "heads"),
            P("heads", None),
        ),
        out_specs=(P("dp", ("blk", "heads"), None), P(("dp", "blk", "heads"), None)),
        check_vma=False,
    )
```

```python
import math

import jax
import jax.numpy as jnp
import numpy as np
from jax import lax
from jax.experimental import pallas as pl
from jax.experimental.pallas import tpu as pltpu
from jax.sharding import PartitionSpec as P

MESH = pl.DeviceIdType.MESH
HD = 128
D = 4096
ROWS = 128
EPSILON = 1e-05
ROPE_BASE = 500000.0
BIG = 1e30
FEATS = 16
KROWS = HD + FEATS
SPAN = 16
OUT = 2048
TILE = 1024
PAD = SPAN
CUT = 18 * 128
WINDOW = 4096
F32 = jnp.float32
BF16 = jnp.bfloat16


def tables():
    frequency = ROPE_BASE ** (-(np.arange(64, dtype=np.float64) * 2.0 / HD))
    frequency = np.concatenate([frequency, frequency])
    base = np.arange(64)[:, None] * float(ROWS) * frequency[None, :]
    step = np.arange(ROWS)[:, None] * frequency[None, :]
    return [f(v).astype(np.float32) for v in (base, step) for f in (np.cos, np.sin)]


def dot(a, b, dims=(((1,), (0,)), ((), ()))):
    return lax.dot_general(a, b, dims, preferred_element_type=F32)


def kernel(
    tok_h, gain, seg, wq_h, wk_h, wv_h, wo_h, base_cos, base_sin, step_cos, step_sin,
    out, gram,
    X, E, tok, WQ, WKV, WO, QE, KV, PKT, GP, GC, GX, GT, GD, AT, AR, PT, RA, RF, ACC, TOP, S0, S1, M0, M1,
    ss, rs, kss, krs, sws, swr, gss, grs, ess, ers, tss, trs, ras, rar, ls,
):
    a, b, h = lax.axis_index("dp"), lax.axis_index("blk"), lax.axis_index("heads")
    x, c = b // 2, b % 2
    y, z = h // 4, h % 4
    zp, zm, zo = (z + 1) % 4, (z + 3) % 4, (z + 2) % 4
    up, down = (a, b, y * 4 + zp), (a, b, y * 4 + zm)
    side = (a, b, (1 - y) * 4 + z)
    far = (1 - a, b, (1 - y) * 4 + z)
    twin = (a, x * 2 + 1 - c, h)
    other = (1 - a, b, h)
    ring = [None] + [(a, ((x + k) % 4) * 2 + c, h) for k in (1, 2, 3)]

    load_tok = pltpu.make_async_copy(tok_h, tok, ls.at[4])
    load_tok.start()
    loads = [
        pltpu.make_async_copy(wk_h, WKV.at[:, 0:HD], ls.at[0]),
        pltpu.make_async_copy(wv_h, WKV.at[:, HD : 2 * HD], ls.at[1]),
        pltpu.make_async_copy(wq_h, WQ, ls.at[2]),
        pltpu.make_async_copy(wo_h, WO.at[0], ls.at[3]),
    ]
    barrier = pltpu.get_barrier_semaphore()
    group = [(a, b, ((y + j // 4) % 2) * 4 + (z + j) % 4) for j in range(1, 8)]
    partners = group + [far, twin, other] + ring[1:]
    for partner in partners:
        pl.semaphore_signal(barrier, inc=1, device_id=partner, device_id_type=MESH)

    load_tok.wait()
    for load in loads:
        load.start()

    def normalise(i, _):
        at = pl.ds(pl.multiple_of(i * 16, 16), 16)
        values = tok[at, :].astype(F32)
        mean_square = jnp.mean(values * values, axis=-1, keepdims=True)
        X[h, at, 0:D] = (values * lax.rsqrt(mean_square + EPSILON) * gain[...]).astype(BF16)
        return 0

    lax.fori_loop(0, ROWS // 16, normalise, 0)
    feature = lax.broadcasted_iota(jnp.int32, (FEATS, ROWS), 0)
    E[h] = jnp.where(feature == seg[...], 1.0, 0.0).astype(BF16)

    pl.semaphore_wait(barrier, len(partners))

    def send(i, src, dst, device):
        return pltpu.make_async_remote_copy(
            src_ref=src, dst_ref=dst, send_sem=ss.at[i], recv_sem=rs.at[i],
            device_id=device, device_id_type=MESH,
        )

    FIRST, LAST = pl.ds(0, CUT), pl.ds(CUT, D - CUT)

    def move(i, g, columns, device, half=None):
        rows = pl.ds(0, ROWS) if half is None else pl.ds(half * 64, 64)
        return send(i, X.at[g, rows, columns], X.at[g, rows, columns], device)

    hs = (1 - y) * 4 + z
    om, op, oo = y * 4 + zm, y * 4 + zp, y * 4 + zo
    nm, np_ = (1 - y) * 4 + zm, (1 - y) * 4 + zp
    y_first = move(0, h, FIRST, side)
    y_last = move(1, h, LAST, side)
    z_first = [move(2, h, FIRST, up), move(3, h, FIRST, down)]
    z_last = [move(4, h, LAST, up), move(5, h, LAST, down)]
    n_first = [move(6, hs, FIRST, up), move(7, hs, FIRST, down)]
    half_first = [move(8, om, FIRST, up, 0), move(9, op, FIRST, down, 1)]
    half_last = [move(10, om, LAST, up, 0), move(11, op, LAST, down, 1)]
    y_near = [move(12, om, LAST, side), move(13, op, LAST, side)]
    y_oppo = [move(14, oo, LAST, side, 0), move(15, oo, LAST, side, 1)]
    half_next = [move(16, nm, FIRST, up, 0), move(17, np_, FIRST, down, 1)]
    gathers = [y_first, y_last, *z_first, *z_last, *n_first, *half_first, *half_last, *y_near, *y_oppo, *half_next]
    for copy in (y_first, *z_last, *z_first, y_last):
        copy.start()
    ids = [
        pltpu.make_async_remote_copy(
            src_ref=E.at[h], dst_ref=E.at[h], send_sem=ess.at[j], recv_sem=ers.at[j],
            device_id=device, device_id_type=MESH,
        )
        for j, device in enumerate(group)
    ]
    for copy in ids:
        copy.start()
    half_rows = pl.ds(pl.multiple_of(c * 256, 256), 256)
    wo_far = send(18, wo_h.at[half_rows], WO.at[1, half_rows], far)
    wo_far.start()
    wo_twin = send(19, WO.at[1, half_rows], WO.at[1, half_rows], twin)

    pads = lax.broadcasted_iota(jnp.int32, (FEATS, HD), 0)
    def clear(slot, _):
        KV[slot] = jnp.zeros((KROWS + HD, HD), BF16)
        KV[slot, HD:KROWS, :] = jnp.where(pads == 8, 1.0, 0.0).astype(BF16)
        return 0

    lax.fori_loop(0, PAD, clear, 0)

    def chunk_of(i):
        stage, second = i // 2, i % 2
        col = jnp.where(stage == 0, jnp.where(second == 0, y, 1 - y),
              jnp.where(stage == 1, y,
              jnp.where(stage == 2, 1 - y, jnp.where(second == 0, y, 1 - y))))
        row = jnp.where(stage == 0, z, jnp.where(stage == 3, zo, jnp.where(second == 0, zm, zp)))
        return col * 4 + row

    def kv_copy(kind, i):
        g = chunk_of(i)
        quad = [x, x, x, (x + 3) % 4, (x + 2) % 4][kind]
        device = [twin, ring[1], ring[2], twin, twin][kind]
        slot = (quad * 2 + c) * 8 + g + PAD
        return pltpu.make_async_remote_copy(
            src_ref=KV.at[slot], dst_ref=KV.at[slot], send_sem=kss.at[kind, i],
            recv_sem=krs.at[kind, i], device_id=device, device_id_type=MESH,
        )

    lane = lax.broadcasted_iota(jnp.int32, (ROWS, HD), 1)
    scale = math.log2(math.e) / math.sqrt(HD)

    def project(items):
        pair = [chunk_of(i) for i in items]
        rows = jnp.concatenate([X[g, :, 0:D] for g in pair], axis=0)
        turns = []
        for g in pair:
            rc = b * 8 + g
            bc, bs = base_cos[pl.ds(rc, 1), :], base_sin[pl.ds(rc, 1), :]
            cosine = bc * step_cos[...] - bs * step_sin[...]
            sine = bs * step_cos[...] + bc * step_sin[...]
            turns.append((cosine, jnp.where(lane < 64, -sine, sine)))
        kv = dot(rows, WKV[...])
        for k, g in enumerate(pair):
            cosine, sine = turns[k]
            slot = b * 8 + g + PAD
            key = kv[k * ROWS : (k + 1) * ROWS, 0:HD]
            key = key * cosine + pltpu.roll(key, 64, 1) * sine
            KV[slot, 0:HD, :] = key.T.astype(BF16)
            KV[slot, HD:KROWS, :] = E[g]
            KV[slot, KROWS : KROWS + HD, :] = kv[k * ROWS : (k + 1) * ROWS, HD : 2 * HD].astype(BF16)
        for i in items:
            for kind in range(3):
                kv_copy(kind, i).start()
        for n in range(2):
            part = dot(rows, WQ[:, n * 256 : (n + 1) * 256])
            for k, g in enumerate(pair):
                cosine, sine = turns[k]
                for m in range(2):
                    head = part[k * ROWS : (k + 1) * ROWS, m * HD : (m + 1) * HD]
                    head = (head * cosine + pltpu.roll(head, 64, 1) * sine) * scale
                    for part_at in range(4):
                        at = part_at * 128 + (n * 2 + m) * 32
                        QE[g, at : at + 32, 0:HD] = head[part_at * 32 : part_at * 32 + 32].astype(BF16)
        for g in pair:
            mine = jnp.concatenate([E[g].astype(F32), jnp.zeros((ROWS - FEATS, ROWS), F32)], axis=0).T
            ext = jnp.where(lane < 8, jnp.where(mine > 0.5, 0.0, -BIG), jnp.where(lane == 8, -BIG, 0.0))
            for m in range(16):
                at = (m // 4) * 32
                QE[g, m * 32 : m * 32 + 32, HD : 2 * HD] = ext[at : at + 32].astype(BF16)

    def forward_kv(items):
        for i in items:
            for kind in (1, 2):
                kv_copy(kind, i).wait_recv()
                kv_copy(kind + 2, i).start()

    for load in loads[:3]:
        load.wait()

    pick_row = lax.broadcasted_iota(jnp.int32, (128, 512), 0)
    pick_col = lax.broadcasted_iota(jnp.int32, (128, 512), 1)
    chosen = (pick_col == (pick_row // 32) * 128 + z * 32 + pick_row % 32)
    chosen = jnp.where(chosen, 1.0, 0.0).astype(BF16)

    def tile_copy(kind, n, src, dst, device):
        return pltpu.make_async_remote_copy(
            src_ref=src, dst_ref=dst, send_sem=gss.at[kind, n], recv_sem=grs.at[kind, n],
            device_id=device, device_id_type=MESH,
        )

    def tile_at(n):
        return pl.ds(pl.multiple_of(n * TILE, TILE), TILE)

    def gram_twin(n):
        return tile_copy(0, n, GP.at[1 - c, :, tile_at(n)], GC.at[:, tile_at(n)], twin)

    def gram_ring(n):
        return [tile_copy(k, n, GP.at[c, pl.ds(pl.multiple_of(((x + k) % 4) * 64, 64), 64), tile_at(n)],
                          GX.at[k - 1, :, tile_at(n)], ring[k]) for k in (1, 2, 3)]

    def gram_other(n):
        rows = pl.ds(pl.multiple_of((1 - a) * 32, 32), 32)
        return tile_copy(4, n, GT.at[rows, tile_at(n)], GD.at[:, tile_at(n)], other)

    def gram_rows(last):
        slabs = [chunk_of(i) for i in ((6, 7) if last else range(6))]
        count = len(slabs) * ROWS
        for group in range(4):
            parts = []
            for n in range(4):
                q = (n % 2) * 8 + (2 * (group % 2) + n // 2) * 2 + group // 2
                at = pl.ds(pl.multiple_of(q * 256 + y * 128, 128), 128)
                parts.append(jnp.concatenate([X[g, :, at] for g in slabs], axis=0))
            taken = jnp.concatenate(parts, axis=1)
            picked = dot(chosen, taken, (((1,), (1,)), ((), ())))
            PKT[group * 128 : (group + 1) * 128, 0:count] = picked.astype(BF16)

        def gram_tile(n, _):
            at = pl.ds(pl.multiple_of(n * TILE, TILE), TILE)
            tile = dot(PKT[:, 0:count], jnp.concatenate([X[g, :, at] for g in slabs], axis=0))
            if last:
                GP[0, :, at] = (tile[0:256] + S0[:, at]).astype(BF16)
                GP[1, :, at] = (tile[256:512] + S1[:, at]).astype(BF16)
                gram_twin(n).start()
            else:
                S0[:, at] = tile[0:256]
                S1[:, at] = tile[256:512]
            return 0

        lax.fori_loop(0, D // TILE, gram_tile, 0)

    def gather_stage(stage, _):
        @pl.when(stage == 0)
        def _():
            for k in (0, 1):
                z_last[k].wait_recv()
                half_last[k].start()
                y_near[k].start()
            y_first.wait_recv()
            for k in (0, 1):
                n_first[k].start()
            for k in (0, 1):
                z_first[k].wait_recv()
                half_first[k].start()
            y_last.wait_recv()
            for copy in ids:
                copy.wait_recv()

        @pl.when(stage == 1)
        def _():
            for k in (0, 1):
                half_last[k].wait_recv()
                y_oppo[k].start()

        @pl.when(stage == 2)
        def _():
            for k in (0, 1):
                n_first[k].wait_recv()
                half_next[k].start()
            for copy in y_near:
                copy.wait_recv()

        project((2 * stage, 2 * stage + 1))

        @pl.when(stage > 0)
        def _():
            forward_kv((2 * stage - 2, 2 * stage - 1))

        return 0

    lax.fori_loop(0, 3, gather_stage, 0)
    gram_rows(False)
    forward_kv((4, 5))

    def gather_last(i, _):
        @pl.when(i == 0)
        def _():
            for copy in half_first:
                copy.wait_recv()

        @pl.when(i == 1)
        def _():
            for copy in (*half_next, *y_oppo):
                copy.wait_recv()

        project((6 + i,))
        return 0

    lax.fori_loop(0, 2, gather_last, 0)
    forward_kv((6,))

    wo_far.wait_recv()
    wo_twin.start()
    gram_rows(True)
    forward_kv((7,))

    def gram_cores():
        def add(n, _):
            gram_twin(n).wait_recv()
            at = tile_at(n)
            GP[c, :, at] = (GP[c, :, at].astype(F32) + GC[:, at].astype(F32)).astype(BF16)
            for copy in gram_ring(n):
                copy.start()
            return 0

        lax.fori_loop(0, D // TILE, add, 0)

    gram_cores()

    def settle(i, _):
        kv_copy(0, i).wait_recv()
        kv_copy(3, i).wait_recv()
        kv_copy(4, i).wait_recv()
        return 0

    lax.fori_loop(0, 8, settle, 0)
    wo_twin.wait_recv()
    loads[3].wait()

    row_in = lax.broadcasted_iota(jnp.int32, (256, HD), 0)
    late = row_in % 32 - lax.broadcasted_iota(jnp.int32, (256, HD), 1)
    second_quarter = row_in >= 128
    blank = jnp.zeros((256 - KROWS, HD), BF16)
    ones = jnp.ones((HD, HD), BF16)
    steps = jnp.minimum(32 // SPAN, (8 * b + 7 + SPAN) // SPAN)

    def queries_of(g, quarters):
        return jnp.concatenate(
            [QE[g, pl.ds(pl.multiple_of(q * 128, 128), 128), :] for q in quarters], axis=0)

    def keys_of(slot):
        return jnp.concatenate([KV[slot, 0:KROWS, :], blank], axis=0)

    def values_of(slot):
        return jnp.concatenate([KV[slot, KROWS : KROWS + HD, :], ones], axis=1)

    def score_first(g, half, S, MX):
        scores = jnp.where(late + jnp.where(second_quarter, half[1], half[0]) * 32 >= 0,
                           dot(queries_of(g, half), keys_of(b * 8 + g + PAD)), -BIG)
        S[:, WINDOW : WINDOW + HD] = scores
        MX[...] = scores

    def score_step(g, half, S, MX, t):
        first = b * 8 + g + PAD - SPAN * (t + 1)
        keys = jnp.concatenate([keys_of(first + j) for j in range(SPAN)], axis=1)
        scores = dot(queries_of(g, half), keys)
        S[:, pl.ds(pl.multiple_of(t * SPAN * HD, SPAN * HD), SPAN * HD)] = scores
        top = MX[...]
        for j in range(SPAN):
            top = jnp.maximum(top, scores[:, j * HD : (j + 1) * HD])
        MX[...] = top

    def mix_first(g, S, MX):
        top = jnp.max(MX[...], axis=1, keepdims=True)
        TOP[...] = jnp.broadcast_to(top, (256, HD))
        probs = jnp.exp2(S[:, WINDOW : WINDOW + HD] - TOP[...]).astype(BF16)
        ACC[...] = dot(probs, values_of(b * 8 + g + PAD))

    def mix_step(g, S, t):
        first = b * 8 + g + PAD - SPAN * (t + 1)
        values = jnp.concatenate([values_of(first + j) for j in range(SPAN)], axis=0)
        scores = S[:, pl.ds(pl.multiple_of(t * SPAN * HD, SPAN * HD), SPAN * HD)]
        top = TOP[...]
        probs = jnp.concatenate(
            [jnp.exp2(scores[:, j * HD : (j + 1) * HD] - top).astype(BF16) for j in range(SPAN)], axis=1)
        ACC[...] += dot(probs, values)

    def mix_last(place):
        mixed = (ACC[:, 0:HD] / ACC[:, HD : 2 * HD]).astype(BF16)
        own, k, second = place
        for m in range(8):
            rows = pl.ds(pl.multiple_of(second * 64 + (m // 4) * 32, 32), 32)
            AT[own * 4 + k, rows, (m % 4) * HD : (m % 4 + 1) * HD] = mixed[m * 32 : m * 32 + 32]

    def both(g, place, S, MX, next_g, next_half, next_S, next_MX):
        mix_first(g, S, MX)
        score_first(next_g, next_half, next_S, next_MX)

        def step(t, _):
            score_step(next_g, next_half, next_S, next_MX, t)
            mix_step(g, S, t)
            return 0

        lax.fori_loop(0, steps, step, 0)
        mix_last(place)

    top, low = pl.ds(0, 64), pl.ds(64, 64)

    def turned(kind, n):
        at = pl.ds(pl.multiple_of(n * OUT, OUT), OUT)
        src = PT.at[1 + kind // 2, low if kind % 2 else top, at]
        dst = [RF.at[0, low, at], RF.at[1, top, at], RF.at[0, top, at], RF.at[1, low, at]][kind]
        return pltpu.make_async_remote_copy(
            src_ref=src, dst_ref=dst, send_sem=tss.at[kind, n], recv_sem=trs.at[kind, n],
            device_id=down if kind % 2 else up, device_id_type=MESH,
        )

    def relayed(which, second, n):
        at = pl.ds(pl.multiple_of(n * OUT, OUT), OUT)
        rows = pl.ds(pl.multiple_of(second * 64 + which * 32, 32), 32)
        to = pl.ds(pl.multiple_of(second * 32, 32), 32)
        return pltpu.make_async_remote_copy(
            src_ref=PT.at[0, rows, at], dst_ref=RA.at[which, to, at], send_sem=ras.at[which, second, n],
            recv_sem=rar.at[which, second, n], device_id=down if which else up, device_id_type=MESH,
        )

    def part_of(k, second):
        row = jnp.where(k == 0, zo, jnp.where(k == 3, z, jnp.where(second == 0, zp, zm)))
        odd = jnp.where(k == 1, 1 - second, second)
        mixed = (k == 1) | (k == 2)
        first = jnp.where(mixed, odd, 2 * second)
        return row, (first, first + jnp.where(mixed, 2, 1))

    def swap(k, second):
        rows = pl.ds(pl.multiple_of(second * 64, 64), 64)
        return pltpu.make_async_remote_copy(
            src_ref=AT.at[k, rows], dst_ref=AR.at[k, rows], send_sem=sws.at[k, second],
            recv_sem=swr.at[k, second], device_id=side, device_id_type=MESH,
        )

    def gram_quads(n):
        for copy in gram_ring(n):
            copy.wait_recv()
        at = tile_at(n)
        total = GP[c, pl.ds(pl.multiple_of(x * 64, 64), 64), at].astype(F32)
        for i in range(3):
            total = total + GX[i, :, at].astype(F32)
        GT[:, at] = total.astype(BF16)
        gram_other(n).start()

    def item_of(i):
        k, j = i // 4, i % 4
        own = jnp.where(k == 0, j % 2, j // 2)
        second = jnp.where(k == 0, j // 2, j % 2)
        row, quarters = part_of(k, second)
        return jnp.where(own == 1, y, 1 - y) * 4 + row, quarters, (own, k, second)

    def project_out(k, rows, n):
        at = pl.ds(pl.multiple_of(n * OUT, OUT), OUT)
        return at, dot(AT[4 + k, rows, :], WO[0, :, at]) + dot(AR[k, rows, :], WO[1, :, at])

    def out_first(second):
        swap(0, second).wait_recv()

        def tile(n, _):
            rows = pl.ds(pl.multiple_of(second * 64, 64), 64)
            at, part = project_out(0, rows, n)
            PT[0, rows, at] = part.astype(BF16)
            relayed(0, second, n).start()
            relayed(1, second, n).start()
            return 0

        lax.fori_loop(0, D // OUT, tile, 0)

    def out_round(k):
        swap(k, 0).wait_recv()
        swap(k, 1).wait_recv()

        def tile(n, _):
            at, part = project_out(k, pl.ds(0, ROWS), n)

            @pl.when(k != 2)
            def _():
                PT[k, :, at] = part.astype(BF16)

            @pl.when(k == 2)
            def _():
                for which, rows in enumerate((top, low)):
                    relayed(which, 0, n).wait_recv()
                    relayed(which, 1, n).wait_recv()
                    first = 64 * which
                    PT[2, rows, at] = (part[first : first + 64] + RA[which, :, at].astype(F32)).astype(BF16)

            for stage in (1, 2):
                @pl.when(k == stage)
                def _(stage=stage):
                    turned(2 * stage - 2, n).start()
                    turned(2 * stage - 1, n).start()

            return 0

        lax.fori_loop(0, D // OUT, tile, 0)

    def item_pair(p, _):
        g0, quarters0, place0 = item_of(2 * p)
        g1, quarters1, place1 = item_of(2 * p + 1)
        g2, quarters2, _place = item_of(jnp.minimum(2 * p + 2, 15))
        both(g0, place0, S0, M0, g1, quarters1, S1, M1)

        @pl.when((p < 2) | (p % 2 == 0))
        def _():
            swap(place0[1], place0[2]).start()

        @pl.when(p == 1)
        def _():
            out_first(0)

        both(g1, place1, S1, M1, g2, quarters2, S0, M0)

        @pl.when((p >= 2) & (p % 2 == 0))
        def _():
            swap(place1[1], place1[2]).start()

        @pl.when(p == 1)
        def _():
            out_first(1)

        @pl.when((p >= 2) & (p < 6))
        def _():
            gram_quads(p - 2)

        @pl.when((p >= 2) & (p % 2 == 1))
        def _():
            out_round(p // 2)

        return 0

    start_g = (1 - y) * 4 + zo
    score_first(start_g, (0, 1), S0, M0)

    def start_step(t, _):
        score_step(start_g, (0, 1), S0, M0, t)
        return 0

    lax.fori_loop(0, steps, start_step, 0)
    lax.fori_loop(0, 8, item_pair, 0)
    mine = pl.ds(pl.multiple_of(a * 32, 32), 32)
    for n in range(D // TILE):
        gram_other(n).wait_recv()
    gram[...] = GT[mine, :].astype(F32) + GD[...].astype(F32)

    def total(n, _):
        at = pl.ds(pl.multiple_of(n * OUT, OUT), OUT)
        for kind in range(4):
            turned(kind, n).wait_recv()
        for q in range(4):
            to, given = pl.ds(q * 32, 32), pl.ds((q % 2) * 64 + (q // 2) * 32, 32)
            out[to, at] = (PT[3, to, at].astype(F32) + RF[0, given, at].astype(F32)
                           + RF[1, given, at].astype(F32)).astype(BF16)
        return 0

    lax.fori_loop(0, D // OUT, total, 0)

    for copy in [*gathers, *ids, wo_far, wo_twin]:
        copy.wait_send()

    def drain(i, _):
        for kind in range(5):
            kv_copy(kind, i).wait_send()
        return 0

    lax.fori_loop(0, 8, drain, 0)

    def drain_gram(n, _):
        for copy in (gram_twin(n), *gram_ring(n), gram_other(n)):
            copy.wait_send()
        return 0

    def drain_turned(n, _):
        for kind in range(4):
            turned(kind, n).wait_send()
        for which in range(2):
            for second in range(2):
                relayed(which, second, n).wait_send()
        return 0

    lax.fori_loop(0, D // OUT, drain_turned, 0)

    lax.fori_loop(0, D // TILE, drain_gram, 0)

    def drain_swap(k, _):
        swap(k, 0).wait_send()
        swap(k, 1).wait_send()
        return 0

    lax.fori_loop(0, 4, drain_swap, 0)


def finish(delta, gram, delta_out, gram_out):
    delta_out[...] = delta[...]
    gram_out[...] = gram[...] * (1.0 / 16384.0)


def per_device(tokens, norm_gain, segment_ids, w_query, w_key, w_value, w_out):
    vmem = pl.BlockSpec(memory_space=pltpu.VMEM)
    hbm = pl.BlockSpec(memory_space=pl.ANY)
    dma = pltpu.SemaphoreType.DMA
    scratch = [
        pltpu.VMEM((8, ROWS, D), BF16),
        pltpu.VMEM((8, FEATS, ROWS), BF16),
        pltpu.VMEM((ROWS, D), BF16),
        pltpu.VMEM((D, 512), BF16),
        pltpu.VMEM((D, 256), BF16),
        pltpu.VMEM((2, 512, D), BF16),
        pltpu.VMEM((8, 512, 256), BF16),
        pltpu.VMEM((64 + PAD, KROWS + HD, HD), BF16),
        pltpu.VMEM((512, 768), BF16),
        pltpu.VMEM((2, 256, D), BF16),
        pltpu.VMEM((256, D), BF16),
        pltpu.VMEM((3, 64, D), BF16),
        pltpu.VMEM((64, D), BF16),
        pltpu.VMEM((32, D), BF16),
        pltpu.VMEM((8, ROWS, 512), BF16),
        pltpu.VMEM((4, ROWS, 512), BF16),
        pltpu.VMEM((4, ROWS, D), BF16),
        pltpu.VMEM((2, 64, D), BF16),
        pltpu.VMEM((2, ROWS, D), BF16),
        pltpu.VMEM((256, 256), F32),
        pltpu.VMEM((256, HD), F32),
        pltpu.VMEM((256, WINDOW + HD), F32),
        pltpu.VMEM((256, WINDOW + HD), F32),
        pltpu.VMEM((256, HD), F32),
        pltpu.VMEM((256, HD), F32),
        dma((40,)),
        dma((40,)),
        dma((5, 8)),
        dma((5, 8)),
        dma((4, 2)),
        dma((4, 2)),
        dma((5, 4)),
        dma((5, 4)),
        dma((7,)),
        dma((7,)),
        dma((4, 2)),
        dma((4, 2)),
        dma((2, 2, 2)),
        dma((2, 2, 2)),
        dma((5,)),
    ]
    delta, gram = pl.pallas_call(
        kernel,
        out_shape=(jax.ShapeDtypeStruct((ROWS, D), BF16), jax.ShapeDtypeStruct((32, D), F32)),
        in_specs=[hbm, vmem, vmem, hbm, hbm, hbm, hbm, vmem, vmem, vmem, vmem],
        out_specs=(vmem, vmem),
        scratch_shapes=scratch,
        compiler_params=pltpu.CompilerParams(
            collective_id=0, has_side_effects=True, vmem_limit_bytes=62 << 20),
        name="sublayer",
    )(tokens[0], norm_gain[None], segment_ids, w_query, w_key, w_value, w_out,
      *[jnp.asarray(t) for t in tables()])
    delta, gram = pl.pallas_call(
        finish,
        out_shape=(jax.ShapeDtypeStruct((ROWS, D), BF16), jax.ShapeDtypeStruct((32, D), F32)),
        grid=(2,),
        in_specs=[pl.BlockSpec((64, D), lambda i: (i, 0)), pl.BlockSpec((16, D), lambda i: (i, 0))],
        out_specs=(pl.BlockSpec((64, D), lambda i: (i, 0)), pl.BlockSpec((16, D), lambda i: (i, 0))),
        name="finish",
    )(delta, gram)
    return delta[None], gram


def solution(mesh):
    return jax.shard_map(
        per_device,
        mesh=mesh,
        in_specs=(
            P("dp", ("blk", "heads"), None),
            P(),
            P("dp", ("blk", "heads")),
            P(None, "heads"),
            P(None, "heads"),
            P(None, "heads"),
            P("heads", None),
        ),
        out_specs=(P("dp", ("blk", "heads"), None), P(("dp", "blk", "heads"), None)),
        check_vma=False,
    )
```
